256 devices in a mesh: tok: 16 (over y, x), head: 16 (over z, core).
Axes of the slice: x: 4, y: 4, z: 8, core: 2. Of those that a mesh axis runs over, the one named last changes fastest.
Arguments:
- queries: bfloat16 [2, 4096, 16, 512], P(None, 'tok', 'head'), may hold values from -6 to 6
- key_rows: bfloat16 [2, 4096, 16, 512], P(None, 'tok', 'head'), may hold values from -6 to 6
- value_rows: bfloat16 [2, 4096, 16, 512], P(None, 'tok', 'head'), may hold values from -6 to 6
- step_sizes: float32 [2, 4096, 16], P(None, 'tok', 'head'), may hold values from 0 to 1, as said below
- out_grads: bfloat16 [2, 4096, 16, 512], P(None, 'tok', 'head'), may hold values from -0.59765625 to 0.59765625
- first_saved: bfloat16 [2, 16, 512, 512], P(None, 'head'), may hold values from -64 to 64
- second_saved: bfloat16 [2, 16, 512, 512], P(None, 'head'), may hold values from -64 to 64
- third_saved: bfloat16 [2, 16, 512, 512], P(None, 'head'), may hold values from -64 to 64
Outputs:
- query_grads: float32 [2, 4096, 16, 512], P(None, 'tok', 'head')
- key_grads: float32 [2, 4096, 16, 512], P(None, 'tok', 'head')
- value_grads: float32 [2, 4096, 16, 512], P(None, 'tok', 'head')
The draws below stay inside these ranges and needn't reach their ends.
Inputs may be any that keep to these rules, and one draw needn't show every extreme that they name: `step_sizes`: positive step sizes.
All inputs are finite; a program needn't handle non-finite values.
Results may differ from the reference program's by a relative error of at most 0.04.
Values may be sent and summed in bfloat16 or wider, within the bound.
A program may use at most 128 MiB of HBM per device.

```python
import math
import jax
import jax.numpy as jnp
from jax import lax

HEADS = 16
DH = 512
FH = 512
BLOCKS = 2
BLOCK = 4096
N_TOK = 16


def weight_law(key, row_count, column_count):
    pieces = jax.random.split(key, 3)
    shape = (BLOCKS, HEADS, row_count, column_count)
    row_scale = jnp.exp(jax.random.uniform(pieces[0], (BLOCKS, HEADS, row_count, 1), jnp.float32, -1.15, 1.15))
    column_scale = jnp.exp(jax.random.uniform(pieces[1], (BLOCKS, HEADS, 1, column_count), jnp.float32, -1.15, 1.15))
    base = jnp.clip(jax.random.normal(pieces[2], shape, jnp.float32), -4.0, 4.0)
    return base * row_scale * column_scale * row_count ** (-0.5)


def draw_first_saved(key, part):
    return weight_law(jax.random.fold_in(key, 11), DH, FH).astype(jnp.bfloat16)


def draw_second_saved(key, part):
    return weight_law(jax.random.fold_in(key, 12), FH, DH).astype(jnp.bfloat16)


def draw_third_saved(key, part):
    return weight_law(jax.random.fold_in(key, 13), DH, FH).astype(jnp.bfloat16)


def draw_step_sizes(key, part):
    base_rate = (BLOCK * DH) ** (-0.5)
    shape = (BLOCKS, BLOCK, HEADS)
    factor = jnp.exp(jax.random.uniform(jax.random.fold_in(key, 21), shape, jnp.float32, math.log(0.5), math.log(4.0)))
    return factor * base_rate


def levels(key, shape, shards, least, largest):
    loudness, own = 1.0, jax.random.fold_in(key, 6)
    for dim, blocks in shards:
        steps = jnp.exp(jax.random.uniform(jax.random.fold_in(own, dim), (blocks,), jnp.float32, least / len(shards), largest / len(shards)))
        loudness = loudness * jnp.repeat(steps, shape[dim] // blocks).reshape([-1 if axis == dim else 1 for axis in range(len(shape))])
    return loudness


def normal_values(own_key, shape, deviation, bound, cuts=(), dtype=jnp.bfloat16):
    drawn = deviation * jax.random.normal(own_key, shape, jnp.float32)
    if cuts:
        drawn = drawn * levels(own_key, shape, cuts, -0.22, 0.18)
    return jnp.clip(drawn, -bound, bound).astype(dtype)


def setup_inputs(seed: int = 0) -> dict:
    arg_keys = jax.random.split(jax.random.key(seed), 9)
    return {
        "queries": normal_values(arg_keys[0], (BLOCKS, BLOCK, HEADS, DH), 1.0, 6.0, ((1, 16), (2, 16))),
        "key_rows": normal_values(arg_keys[1], (BLOCKS, BLOCK, HEADS, DH), 1.0, 6.0, ((1, 16), (2, 16))),
        "value_rows": normal_values(arg_keys[2], (BLOCKS, BLOCK, HEADS, DH), 1.0, 6.0, ((1, 16), (2, 16))),
        "step_sizes": draw_step_sizes(jax.random.fold_in(arg_keys[8], 71), 0),
        "out_grads": normal_values(arg_keys[4], (BLOCKS, BLOCK, HEADS, DH), 0.1, 0.59765625, ((1, 16), (2, 16))),
        "first_saved": draw_first_saved(jax.random.fold_in(arg_keys[8], 71), 0),
        "second_saved": draw_second_saved(jax.random.fold_in(arg_keys[8], 71), 0),
        "third_saved": draw_third_saved(jax.random.fold_in(arg_keys[8], 71), 0),
    }


epsilon = 1e-06

def product(pattern, left_side, right_side):
    return jnp.einsum(pattern, left_side.astype(jnp.float32), right_side.astype(jnp.float32))

def add_terms(first_terms, second_terms):
    return tuple((paired[0] + paired[1] for paired in zip(first_terms, second_terms)))

def column_norm(matrix):
    return jnp.sqrt(lax.optimization_barrier(jnp.sum(matrix * matrix, axis=1)) + epsilon)

def forward_terms(weights, key_vecs, value_vecs, step_vecs):
    first_weight, second_weight, third_weight = weights
    gate_in = product('thd,hdf->thf', key_vecs, first_weight)
    lift_in = product('thd,hdf->thf', key_vecs, third_weight)
    squash = jax.nn.sigmoid(gate_in)
    activated = gate_in * squash
    gated_hidden = (activated * lift_in).astype(jnp.bfloat16)
    targets = (step_vecs[..., None] * value_vecs.astype(jnp.float32)).astype(jnp.bfloat16)
    back_hidden = product('thd,hfd->thf', targets, second_weight)
    slopes = squash * (1.0 + gate_in * (1.0 - squash))
    grad_gate = (back_hidden * lift_in * slopes).astype(jnp.bfloat16)
    grad_lift = (back_hidden * activated).astype(jnp.bfloat16)
    return (gate_in, lift_in, squash, activated, gated_hidden, targets, back_hidden, slopes, grad_gate, grad_lift)

def apply_back(matrices, query_vecs, grad_vecs):
    first_weight, second_weight, third_weight = matrices
    gate_in = product('thd,hdf->thf', query_vecs, first_weight)
    lift_in = product('thd,hdf->thf', query_vecs, third_weight)
    squash = jax.nn.sigmoid(gate_in)
    activated = gate_in * squash
    gated_hidden = (activated * lift_in).astype(jnp.bfloat16)
    back_hidden = product('thd,hfd->thf', grad_vecs, second_weight)
    slopes = squash * (1.0 + gate_in * (1.0 - squash))
    grad_gate = (back_hidden * lift_in * slopes).astype(jnp.bfloat16)
    grad_lift = (back_hidden * activated).astype(jnp.bfloat16)
    query_out = product('thf,hdf->thd', grad_gate, first_weight) + product('thf,hdf->thd', grad_lift, third_weight)
    pieces = (product('tha,thb->hab', query_vecs, grad_gate), product('tha,thb->hab', gated_hidden, grad_vecs), product('tha,thb->hab', query_vecs, grad_lift))
    return (query_out, pieces)

def update_back(weights, key_vecs, step_vecs, forward, moves):
    first_weight, second_weight, third_weight = weights
    gate_in, lift_in, squash, activated, gated_hidden, targets, back_hidden, slopes, grad_gate, grad_lift = forward
    first_move, second_move, third_move = moves
    gated_back = product('thd,hfd->thf', targets, second_move)
    target_back = product('thf,hfd->thd', gated_hidden, second_move)
    first_back = product('thd,hdf->thf', key_vecs, first_move)
    third_back = product('thd,hdf->thf', key_vecs, third_move)
    curves = squash * (1.0 - squash) * (2.0 + gate_in * (1.0 - 2.0 * squash))
    hidden_back = (first_back * lift_in * slopes + third_back * activated).astype(jnp.bfloat16)
    gate_back = ((gated_back * lift_in + third_back * back_hidden) * slopes + first_back * back_hidden * lift_in * curves).astype(jnp.bfloat16)
    lift_back = (first_back * back_hidden * slopes + gated_back * activated).astype(jnp.bfloat16)
    target_back = target_back + product('thf,hfd->thd', hidden_back, second_weight)
    value_out = step_vecs[..., None] * target_back
    key_out = product('thf,hdf->thd', grad_gate, first_move) + product('thf,hdf->thd', grad_lift, third_move) + product('thf,hdf->thd', gate_back, first_weight) + product('thf,hdf->thd', lift_back, third_weight)
    return (key_out, value_out, (gate_back, hidden_back, lift_back))

def start_terms(key_vecs, forward, backs):
    gate_back, hidden_back, lift_back = backs
    return (product('tha,thb->hab', key_vecs, gate_back), product('tha,thb->hab', hidden_back, forward[5]), product('tha,thb->hab', key_vecs, lift_back))

def renorm_terms(cotangents, matrices, weights, kept_norms, summed_norms, inner_sums):
    moves = []
    direct = []
    for cotangent, matrix, weight, kept, summed, inner in zip(cotangents, matrices, weights, kept_norms, summed_norms, inner_sums):
        factor = kept / summed
        moves.append(cotangent * factor[:, None, :] - matrix * (factor * inner / (summed * summed))[:, None, :])
        direct.append(weight.astype(jnp.float32) * (inner / (summed * kept))[:, None, :])
    return (tuple(moves), tuple(direct))

def shard_total(left_side, right_side):
    split_left = left_side.reshape((N_TOK, -1) + left_side.shape[1:]).astype(jnp.float32)
    split_right = right_side.reshape((N_TOK, -1) + right_side.shape[1:]).astype(jnp.float32)
    terms_each = jnp.einsum('stha,sthb->shab', split_left, split_right)
    rounded = lax.optimization_barrier(terms_each.astype(jnp.bfloat16))
    return lax.optimization_barrier(jnp.sum(rounded.astype(jnp.float32), axis=0))

def restate(weights, key_vecs, value_vecs, step_vecs):
    forward = forward_terms(weights, key_vecs, value_vecs, step_vecs)
    changes = (shard_total(key_vecs, forward[8]), shard_total(forward[4], forward[5]), shard_total(key_vecs, forward[9]))
    matrices = tuple((weight.astype(jnp.float32) + change for weight, change in zip(weights, changes)))
    kept_norms = tuple((column_norm(weight.astype(jnp.float32)) for weight in weights))
    summed_norms = tuple((column_norm(matrix) for matrix in matrices))
    renormed = tuple((matrix * (kept / summed)[:, None, :] for matrix, kept, summed in zip(matrices, kept_norms, summed_norms)))
    return (forward, matrices, kept_norms, summed_norms, renormed)

def renorm_back(cotangents, matrices, weights, kept_norms, summed_norms):
    inner_sums = tuple((lax.optimization_barrier(jnp.sum(cotangent * matrix, axis=1)) for cotangent, matrix in zip(cotangents, matrices)))
    return renorm_terms(cotangents, matrices, weights, kept_norms, summed_norms, inner_sums)

def one_head(pieces):
    query_all, key_all, value_all, step_all, grad_all, first_all, second_all, third_all = pieces
    queries = query_all[:, :, None, :]
    key_vecs = key_all[:, :, None, :]
    value_vecs = value_all[:, :, None, :]
    step_vecs = step_all[:, :, None]
    grad_vecs = grad_all[:, :, None, :]
    later = (first_all[1][None], second_all[1][None], third_all[1][None])
    earlier = (first_all[0][None], second_all[0][None], third_all[0][None])
    forward_late, matrices_late, kept_late, summed_late, renormed_late = restate(later, key_vecs[1], value_vecs[1], step_vecs[1])
    applied_late = tuple((matrix.astype(jnp.bfloat16) for matrix in renormed_late))
    query_late, pieces_late = apply_back(applied_late, queries[1], grad_vecs[1])
    moves_late, direct_late = renorm_back(pieces_late, matrices_late, later, kept_late, summed_late)
    rounded_late = tuple((move.astype(jnp.bfloat16) for move in moves_late))
    key_late, value_late, backs_late = update_back(later, key_vecs[1], step_vecs[1], forward_late, rounded_late)
    starts_late = start_terms(key_vecs[1], forward_late, backs_late)
    query_early, pieces_early = apply_back(later, queries[0], grad_vecs[0])
    state_cot = add_terms(add_terms(add_terms(pieces_early, starts_late), moves_late), direct_late)
    forward_early, matrices_early, kept_early, summed_early, unused_new = restate(earlier, key_vecs[0], value_vecs[0], step_vecs[0])
    moves_early, unused_direct = renorm_back(state_cot, matrices_early, earlier, kept_early, summed_early)
    rounded_early = tuple((move.astype(jnp.bfloat16) for move in moves_early))
    key_early, value_early, unused_backs = update_back(earlier, key_vecs[0], step_vecs[0], forward_early, rounded_early)
    return (jnp.stack([query_early, query_late])[:, :, 0, :], jnp.stack([key_early, key_late])[:, :, 0, :], jnp.stack([value_early, value_late])[:, :, 0, :])

def reference(queries, key_rows, value_rows, step_sizes, out_grads, first_saved, second_saved, third_saved):
    stacked = (jnp.moveaxis(queries, 2, 0), jnp.moveaxis(key_rows, 2, 0), jnp.moveaxis(value_rows, 2, 0), jnp.moveaxis(step_sizes, 2, 0), jnp.moveaxis(out_grads, 2, 0), jnp.moveaxis(first_saved, 1, 0), jnp.moveaxis(second_saved, 1, 0), jnp.moveaxis(third_saved, 1, 0))
    results = lax.map(one_head, stacked)
    return (jnp.moveaxis(results[0], 0, 2), jnp.moveaxis(results[1], 0, 2), jnp.moveaxis(results[2], 0, 2))
```

```python
import functools

import jax
import jax.numpy as jnp
from jax import lax
from jax.experimental import pallas as pl
from jax.experimental.pallas import tpu as pltpu
from jax.sharding import PartitionSpec as P

EPSILON = 1e-06
MESH = pl.DeviceIdType.MESH
F32, BF16 = jnp.float32, jnp.bfloat16
SIDE = 4
TOK, DIM = 256, 512
HALF = DIM // 2
BAND = HALF // SIDE
OWN = BAND // SIDE
CHUNK = 16
D_LATE, C_LATE, C_EARLY, D_EARLY = range(4)
R_LATE, M_LATE, M_EARLY = range(3)


def nn(left, right):
    return lax.dot_general(left, right, (((1,), (0,)), ((), ())), preferred_element_type=F32)


def nt(left, right):
    return lax.dot_general(left, right, (((1,), (1,)), ((), ())), preferred_element_type=F32)


def tn(left, right):
    return lax.dot_general(left, right, (((0,), (0,)), ((), ())), preferred_element_type=F32)


def kernel(
    q_any, k_any, v_any, s_any, g_any, w1_any, w2_any, w3_any,
    query_any, key_any, value_any,
    q, k, v, s, g, w,
    a_in, b_in, back, squash, gated, target, ga, gb,
    a_out, b_out, back_out, gated_out, ga_out, gb_out,
    first_back, third_back, gated_back, gate_back, hidden_back, lift_back,
    c_early, own_w, own_p, own_add, kept, summed,
    snd, got1, mid, got2, whole, out,
    in_sem, out_sem,
    rs1_send, rs1_recv, rs2_send, rs2_recv, ag1_send, ag1_recv, ag2_send, ag2_recv,
):
    tok = lax.axis_index("tok")
    x, y = lax.rem(tok, SIDE), tok // SIDE
    along_x = [(y * SIDE + lax.rem(x + d, SIDE), lax.rem(x + d, SIDE)) for d in range(1, SIDE)]
    along_y = [(lax.rem(y + d, SIDE) * SIDE + x, lax.rem(y + d, SIDE)) for d in range(1, SIDE)]

    weights_any = (w1_any, w2_any, w3_any)
    loads = {}

    def load(name, source, place):
        copy = pltpu.make_async_copy(source, place, in_sem.at[len(loads)])
        copy.start()
        loads[name] = copy

    def arrived(*names):
        for name in names:
            loads[name].wait()

    load("s", s_any, s)
    for b in (1, 0):
        load(("k", b), k_any.at[b], k.at[b])
        load(("w", b, 0), weights_any[0].at[b], w.at[b, 0])
        load(("w", b, 2), weights_any[2].at[b], w.at[b, 2])
        load(("v", b), v_any.at[b], v.at[b])
        load(("w", b, 1), weights_any[1].at[b], w.at[b, 1])
    for b in (0, 1):
        load(("q", b), q_any.at[b], q.at[b])
        load(("g", b), g_any.at[b], g.at[b])

    barrier = pltpu.get_barrier_semaphore()
    for peer, _ in along_x + along_y:
        pl.semaphore_signal(barrier, inc=1, device_id={"tok": peer}, device_id_type=MESH)

    started = {}

    def send(name, source, place, send_sem, recv_sem, peer):
        copy = pltpu.make_async_remote_copy(
            src_ref=source, dst_ref=place, send_sem=send_sem, recv_sem=recv_sem,
            device_id={"tok": peer}, device_id_type=MESH,
        )
        copy.start()
        started.setdefault(name, []).append(copy)

    def received(name):
        for copy in started[name]:
            copy.wait_recv()

    def rows(start, size):
        return pl.ds(pl.multiple_of(start, OWN), size)

    def rs_start(c, m):
        for d in range(SIDE - 1):
            for half, (peer, at) in ((0, along_x[d]), (1, along_y[d])):
                send(("rs1", c, m, half), snd.at[c, m, rows(half * HALF + at * BAND, BAND)], got1.at[c, m, half, d],
                     rs1_send.at[c, m, half, d], rs1_recv.at[c, m, half, d], peer)

    def rs_middle(c, m):
        for half, mine, peers in ((0, x, along_y), (1, y, along_x)):
            received(("rs1", c, m, half))
            total = snd[c, m, rows(half * HALF + mine * BAND, BAND), :].astype(F32)
            for d in range(SIDE - 1):
                total = total + got1[c, m, half, d].astype(F32)
            mid[c, m, half] = total.astype(BF16)
            for d, (peer, at) in enumerate(peers):
                send(("rs2", c, m, half), mid.at[c, m, half, rows(at * OWN, OWN)], got2.at[c, m, half, d],
                     rs2_send.at[c, m, half, d], rs2_recv.at[c, m, half, d], peer)

    def rs_end(c, m):
        parts = []
        for half, mine in ((0, y), (1, x)):
            received(("rs2", c, m, half))
            total = mid[c, m, half, rows(mine * OWN, OWN), :].astype(F32)
            for d in range(SIDE - 1):
                total = total + got2[c, m, half, d].astype(F32)
            parts.append(total)
        return jnp.concatenate(parts, axis=0)

    own_rows = (x * BAND + y * OWN, HALF + y * BAND + x * OWN)
    band_rows = (x * BAND, HALF + y * BAND)

    def ag_start(c, m, value):
        for half, peers in ((0, along_y), (1, along_x)):
            whole[c, m, rows(own_rows[half], OWN), :] = value[half * OWN:(half + 1) * OWN]
            for d, (peer, _) in enumerate(peers):
                place = whole.at[c, m, rows(own_rows[half], OWN)]
                send(("ag1", c, m, half), place, place, ag1_send.at[c, m, half, d], ag1_recv.at[c, m, half, d], peer)

    def ag_middle(c, m):
        for half, peers in ((0, along_x), (1, along_y)):
            received(("ag1", c, m, half))
            for d, (peer, _) in enumerate(peers):
                place = whole.at[c, m, rows(band_rows[half], BAND)]
                send(("ag2", c, m, half), place, place, ag2_send.at[c, m, half, d], ag2_recv.at[c, m, half, d], peer)

    def ag_end(c, m):
        for half in (0, 1):
            received(("ag2", c, m, half))

    def by_chunk(step):
        def body(i, carry):
            step(rows(i * CHUNK, CHUNK))
            return carry

        lax.fori_loop(0, TOK // CHUNK, body, 0)

    def forward_inner(b):
        a_in[b] = nn(k[b], w[b, 0])
        b_in[b] = nn(k[b], w[b, 2])

    def forward_target(b):
        step = jnp.broadcast_to(s[b], (128, TOK)).T
        for j in range(DIM // 128):
            lanes = slice(j * 128, (j + 1) * 128)
            target[b, :, lanes] = (step * v[b, :, lanes].astype(F32)).astype(BF16)

    def forward_rest(b):
        back[b] = nt(target[b], w[b, 1])

        def step(r):
            gate, lift, hidden = a_in[b, r, :], b_in[b, r, :], back[b, r, :]
            sg = jax.nn.sigmoid(gate)
            activated = gate * sg
            slope = sg * (1.0 + gate * (1.0 - sg))
            squash[b, r, :] = sg
            gated[b, r, :] = (activated * lift).astype(BF16)
            ga[b, r, :] = (hidden * lift * slope).astype(BF16)
            gb[b, r, :] = (hidden * activated).astype(BF16)

        by_chunk(step)

    def update_term(b, m):
        if m == 0:
            return tn(ga[b], k[b])
        if m == 1:
            return tn(target[b], gated[b])
        return tn(gb[b], k[b])

    row_of = lax.broadcasted_iota(jnp.int32, (2 * OWN, DIM), 0)
    col_of = lax.broadcasted_iota(jnp.int32, (2 * OWN, DIM), 1)
    wanted = jnp.where(row_of < OWN, own_rows[0] + row_of, own_rows[1] + row_of - OWN)
    picker = jnp.where(col_of == wanted, 1.0, 0.0).astype(BF16)

    def own_columns(b, m):
        mine = nt(picker, w[b, m])
        own_w[b, m] = mine
        kept[b, m] = jnp.broadcast_to(jnp.sqrt(jnp.sum(mine * mine, axis=1, keepdims=True) + EPSILON), (2 * OWN, 128))

    def own_update(b, m, change):
        total = own_w[b, m] + change
        own_p[b, m] = total
        summed[b, m] = jnp.broadcast_to(jnp.sqrt(jnp.sum(total * total, axis=1, keepdims=True) + EPSILON), (2 * OWN, 128))
        return total * (kept[b, m, :, :1] / summed[b, m, :, :1])

    def renorm_back(b, m, cotangent):
        matrix, before, after = own_p[b, m], kept[b, m, :, :1], summed[b, m, :, :1]
        inner = jnp.sum(cotangent * matrix, axis=1, keepdims=True)
        factor = before / after
        move = cotangent * factor - matrix * (factor * inner / (after * after))
        return move, own_w[b, m] * (inner / (after * before))

    def output_step():
        def step(r):
            gate, lift, hidden = a_out[r, :], b_out[r, :], back_out[r, :]
            sg = jax.nn.sigmoid(gate)
            activated = gate * sg
            slope = sg * (1.0 + gate * (1.0 - sg))
            gated_out[r, :] = (activated * lift).astype(BF16)
            ga_out[r, :] = (hidden * lift * slope).astype(BF16)
            gb_out[r, :] = (hidden * activated).astype(BF16)

        by_chunk(step)

    def store_out(i, b, value):
        for j in range(DIM // 128):
            out[i, pl.ds(b * TOK * 4 + j, TOK, stride=4), :] = value[:, j * 128:(j + 1) * 128]
        place = pl.ds(b * TOK * 4, TOK * 4)
        target_any = (query_any, key_any, value_any)[i]
        copy = pltpu.make_async_copy(out.at[i, place], target_any.at[place], out_sem.at[i, b])
        copy.start()
        return copy

    stores = []

    def update_step(b):
        def step(r):
            gate, lift, hidden, sg = a_in[b, r, :], b_in[b, r, :], back[b, r, :], squash[b, r, :]
            fb, tb, gdb = first_back[r, :], third_back[r, :], gated_back[r, :]
            activated = gate * sg
            rest = 1.0 - sg
            slope = sg * (1.0 + gate * rest)
            curve = sg * rest * (2.0 + gate * (1.0 - 2.0 * sg))
            hidden_back[r, :] = (fb * lift * slope + tb * activated).astype(BF16)
            gate_back[r, :] = ((gdb * lift + tb * hidden) * slope + fb * hidden * lift * curve).astype(BF16)
            lift_back[r, :] = (fb * hidden * slope + gdb * activated).astype(BF16)

        by_chunk(step)

    def update_inner(b, c, m):
        if m == 0:
            first_back[...] = nt(k[b], whole[c, 0])
        elif m == 1:
            gated_back[...] = nn(target[b], whole[c, 1])
        else:
            third_back[...] = nt(k[b], whole[c, 2])

    def value_result(b, c):
        total = nt(gated[b], whole[c, 1]) + nn(hidden_back[...], w[b, 1])
        step = jnp.broadcast_to(s[b], (128, TOK)).T
        return jnp.concatenate([total[:, j * 128:(j + 1) * 128] * step for j in range(DIM // 128)], axis=1)

    def key_result(b, c):
        return (nn(ga[b], whole[c, 0]) + nn(gb[b], whole[c, 2])
                + nt(gate_back[...], w[b, 0]) + nt(lift_back[...], w[b, 2]))

    order = (0, 2, 1)
    arrived(("k", 1), ("w", 1, 0), ("w", 1, 2))
    forward_inner(1)
    arrived("s", ("v", 1), ("w", 1, 1))
    forward_target(1)
    forward_rest(1)
    pl.semaphore_wait(barrier, 2 * (SIDE - 1))
    for m in order:
        snd[D_LATE, m] = update_term(1, m).astype(BF16)
        rs_start(D_LATE, m)
    for m in order:
        own_columns(1, m)
    arrived(("k", 0), ("w", 0, 0), ("w", 0, 2))
    forward_inner(0)
    arrived(("v", 0), ("w", 0, 1))
    forward_target(0)
    forward_rest(0)
    for m in order:
        rs_middle(D_LATE, m)
    for m in order:
        own_columns(0, m)
    for m in order:
        renormed = own_update(1, m, rs_end(D_LATE, m))
        ag_start(R_LATE, m, renormed.astype(BF16))
    arrived(("q", 0), ("g", 0))
    a_out[...] = nn(q[0], w[1, 0])
    b_out[...] = nn(q[0], w[1, 2])
    for m in order:
        ag_middle(R_LATE, m)
    back_out[...] = nt(g[0], w[1, 1])
    output_step()
    c_early[0] = tn(ga_out[...], q[0])
    c_early[1] = tn(g[0], gated_out[...])
    c_early[2] = tn(gb_out[...], q[0])
    for m in order:
        snd[D_EARLY, m] = update_term(0, m).astype(BF16)
    stores.append(store_out(0, 0, nt(ga_out[...], w[1, 0]) + nt(gb_out[...], w[1, 2])))
    arrived(("q", 1), ("g", 1))
    ag_end(R_LATE, 0)
    a_out[...] = nt(q[1], whole[R_LATE, 0])
    ag_end(R_LATE, 2)
    b_out[...] = nt(q[1], whole[R_LATE, 2])
    ag_end(R_LATE, 1)
    back_out[...] = nn(g[1], whole[R_LATE, 1])
    rs_start(D_EARLY, 0)
    output_step()
    snd[C_LATE, 0] = tn(ga_out[...], q[1]).astype(BF16)
    rs_start(C_LATE, 0)
    snd[C_LATE, 2] = tn(gb_out[...], q[1]).astype(BF16)
    rs_start(C_LATE, 2)
    snd[C_LATE, 1] = tn(g[1], gated_out[...]).astype(BF16)
    rs_start(C_LATE, 1)
    stores.append(store_out(0, 1, nn(ga_out[...], whole[R_LATE, 0]) + nn(gb_out[...], whole[R_LATE, 2])))
    for m in order:
        rs_middle(C_LATE, m)
    for m in order:
        move, direct = renorm_back(1, m, rs_end(C_LATE, m))
        own_add[m] = move + direct
        ag_start(M_LATE, m, move.astype(BF16))
    for m in order:
        ag_middle(M_LATE, m)
    rs_middle(D_EARLY, 0)
    for m in order:
        ag_end(M_LATE, m)
        update_inner(1, M_LATE, m)
    rs_start(D_EARLY, 2)
    rs_start(D_EARLY, 1)
    update_step(1)
    snd[C_EARLY, 0] = (c_early[0] + tn(gate_back[...], k[1])).astype(BF16)
    rs_start(C_EARLY, 0)
    snd[C_EARLY, 2] = (c_early[2] + tn(lift_back[...], k[1])).astype(BF16)
    rs_start(C_EARLY, 2)
    snd[C_EARLY, 1] = (c_early[1] + tn(target[1], hidden_back[...])).astype(BF16)
    rs_start(C_EARLY, 1)
    rs_middle(D_EARLY, 2)
    rs_middle(D_EARLY, 1)
    stores.append(store_out(1, 1, key_result(1, M_LATE)))
    stores.append(store_out(2, 1, value_result(1, M_LATE)))
    for m in order:
        rs_middle(C_EARLY, m)
    for m in order:
        own_update(0, m, rs_end(D_EARLY, m))
    for m in order:
        move, _ = renorm_back(0, m, rs_end(C_EARLY, m) + own_add[m])
        ag_start(M_EARLY, m, move.astype(BF16))
    for m in order:
        ag_middle(M_EARLY, m)
    for m in order:
        ag_end(M_EARLY, m)
        update_inner(0, M_EARLY, m)
    update_step(0)
    stores.append(store_out(1, 0, key_result(0, M_EARLY)))
    stores.append(store_out(2, 0, value_result(0, M_EARLY)))
    for copies in started.values():
        for copy in copies:
            copy.wait_send()
    for copy in stores:
        copy.wait()


def local(queries, key_rows, value_rows, step_sizes, out_grads, first_saved, second_saved, third_saved):
    vectors = [a.reshape(2, TOK, DIM) for a in (queries, key_rows, value_rows)]
    matrices = [a.reshape(2, DIM, DIM) for a in (first_saved, second_saved, third_saved)]
    anywhere = pl.BlockSpec(memory_space=pl.ANY)

    def vmem(*shape, dtype=F32):
        return pltpu.VMEM(shape, dtype)

    sem = pltpu.SemaphoreType.DMA
    result = pl.pallas_call(
        kernel,
        out_shape=[jax.ShapeDtypeStruct((2 * TOK * DIM // 128, 128), F32)] * 3,
        in_specs=[anywhere] * 8,
        out_specs=[anywhere] * 3,
        scratch_shapes=[
            vmem(2, TOK, DIM, dtype=BF16), vmem(2, TOK, DIM, dtype=BF16), vmem(2, TOK, DIM, dtype=BF16),
            vmem(2, 1, TOK), vmem(2, TOK, DIM, dtype=BF16), vmem(2, 3, DIM, DIM, dtype=BF16),
            *[vmem(2, TOK, DIM)] * 4,
            *[vmem(2, TOK, DIM, dtype=BF16)] * 4,
            *[vmem(TOK, DIM)] * 3,
            *[vmem(TOK, DIM, dtype=BF16)] * 3,
            *[vmem(TOK, DIM)] * 3,
            *[vmem(TOK, DIM, dtype=BF16)] * 3,
            vmem(3, DIM, DIM),
            vmem(2, 3, 2 * OWN, DIM), vmem(2, 3, 2 * OWN, DIM), vmem(3, 2 * OWN, DIM),
            vmem(2, 3, 2 * OWN, 128), vmem(2, 3, 2 * OWN, 128),
            vmem(4, 3, DIM, DIM, dtype=BF16),
            vmem(4, 3, 2, SIDE - 1, BAND, DIM, dtype=BF16),
            vmem(4, 3, 2, BAND, DIM, dtype=BF16),
            vmem(4, 3, 2, SIDE - 1, OWN, DIM, dtype=BF16),
            vmem(3, 3, DIM, DIM, dtype=BF16),
            vmem(3, 2 * TOK * DIM // 128, 128),
            sem((17,)), sem((3, 2)),
            *[sem((4, 3, 2, SIDE - 1))] * 4,
            *[sem((3, 3, 2, SIDE - 1))] * 4,
        ],
        compiler_params=pltpu.CompilerParams(
            collective_id=0, has_side_effects=True, vmem_limit_bytes=60 * 2**20
        ),
        cost_estimate=pl.CostEstimate(flops=7 * 10**9, bytes_accessed=9 * 10**6, transcendentals=10**6),
    )(*vectors, step_sizes.reshape(2, 1, TOK), out_grads.reshape(2, TOK, DIM), *matrices)
    return tuple(part.reshape(2, TOK, 1, DIM) for part in result)


def solution(mesh):
    vectors, steps, matrices = P(None, "tok", "head", None), P(None, "tok", "head"), P(None, "head", None, None)
    return jax.shard_map(
        local,
        mesh=mesh,
        in_specs=(vectors, vectors, vectors, steps, vectors, matrices, matrices, matrices),
        out_specs=(vectors, vectors, vectors),
        check_vma=False,
    )
```

```python
import functools

import jax
import jax.numpy as jnp
from jax import lax
from jax.experimental import pallas as pl
from jax.experimental.pallas import tpu as pltpu
from jax.sharding import PartitionSpec as P

EPSILON = 1e-06
MESH = pl.DeviceIdType.MESH
F32, BF16 = jnp.float32, jnp.bfloat16
SIDE = 4
TOK, DIM = 256, 512
HALF = DIM // 2
BAND = HALF // SIDE
OWN = BAND // SIDE
PARTS = 4
CHUNK = 16
D_LATE, C_LATE, C_EARLY, D_EARLY = range(4)
R_LATE, M_LATE, M_EARLY = range(3)


def nn(left, right):
    return lax.dot_general(left, right, (((1,), (0,)), ((), ())), preferred_element_type=F32)


def nt(left, right):
    return lax.dot_general(left, right, (((1,), (1,)), ((), ())), preferred_element_type=F32)


def tn(left, right):
    return lax.dot_general(left, right, (((0,), (0,)), ((), ())), preferred_element_type=F32)


def kernel(
    q_any, k_any, v_any, s_any, g_any, w1_any, w2_any, w3_any,
    query_any, key_any, value_any,
    q, k, v, s, g, w,
    a_in, b_in, back, factors, gated, target, ga, gb,
    a_out, b_out, back_out, gated_out, ga_out, gb_out,
    first_back, third_back, gated_back, gate_back, hidden_back, lift_back,
    c_early, own_w, own_p, own_add, kept, summed,
    snd, passing, passed, got1, mid, got2, whole, out,
    in_sem, out_sem, send_sem, recv_sem,
):
    tok = lax.axis_index("tok")
    x, y = lax.rem(tok, SIDE), tok // SIDE
    along_x = [(y * SIDE + lax.rem(x + d, SIDE), lax.rem(x + d, SIDE)) for d in range(1, SIDE)]
    along_y = [(lax.rem(y + d, SIDE) * SIDE + x, lax.rem(y + d, SIDE)) for d in range(1, SIDE)]

    weights_any = (w1_any, w2_any, w3_any)
    loads = {}

    def load(name, source, place):
        copy = pltpu.make_async_copy(source, place, in_sem.at[len(loads)])
        copy.start()
        loads[name] = copy

    def arrived(*names):
        for name in names:
            loads[name].wait()

    load("s", s_any, s)
    for b in (1, 0):
        load(("k", b), k_any.at[b], k.at[b])
        load(("w", b, 0), weights_any[0].at[b], w.at[b, 0])
        load(("w", b, 2), weights_any[2].at[b], w.at[b, 2])
        load(("v", b), v_any.at[b], v.at[b])
        load(("w", b, 1), weights_any[1].at[b], w.at[b, 1])
    for b in (0, 1):
        load(("q", b), q_any.at[b], q.at[b])
        load(("g", b), g_any.at[b], g.at[b])

    barrier = pltpu.get_barrier_semaphore()
    for peer, _ in along_x + along_y:
        pl.semaphore_signal(barrier, inc=1, device_id={"tok": peer}, device_id_type=MESH)

    started = {}
    sem_count = [0]

    def send(name, source, place, peer):
        n = sem_count[0]
        sem_count[0] = n + 1
        copy = pltpu.make_async_remote_copy(
            src_ref=source, dst_ref=place, send_sem=send_sem.at[n], recv_sem=recv_sem.at[n],
            device_id={"tok": peer}, device_id_type=MESH,
        )
        copy.start()
        started.setdefault(name, []).append(copy)

    def received(name):
        for copy in started[name]:
            copy.wait_recv()

    def rows(start, size):
        return pl.ds(pl.multiple_of(start, OWN), size)

    def ring(peers):
        return peers[0], peers[1], peers[2]

    firsts = ((0, x, along_x, along_y), (1, y, along_y, along_x))
    UPPER, LOWER = 0, BAND // 2

    def rs_start(c, m):
        for half, _, peers, _ in firsts:
            (right, at_right), (_, at_far), (left, at_left) = ring(peers)
            far, near_right, near_left = (half * HALF + at * BAND for at in (at_far, at_right, at_left))
            send(("far", c, m, half, 0), snd.at[c, m, rows(far + UPPER, BAND // 2)], passing.at[c, m, half, 0], right)
            send(("far", c, m, half, 1), snd.at[c, m, rows(far + LOWER, BAND // 2)], passing.at[c, m, half, 1], left)
            send(("near", c, m, half), snd.at[c, m, rows(near_right + LOWER, BAND // 2)],
                 got1.at[c, m, half, 0, pl.ds(LOWER, BAND // 2)], right)
            send(("near", c, m, half), snd.at[c, m, rows(near_left + UPPER, BAND // 2)],
                 got1.at[c, m, half, 1, pl.ds(UPPER, BAND // 2)], left)

    def rs_relay(c, m):
        for half, _, peers, _ in firsts:
            (right, at_right), _, (left, at_left) = ring(peers)
            for side, peer, at, part in ((0, right, at_right, UPPER), (1, left, at_left, LOWER)):
                received(("far", c, m, half, side))
                mine = snd[c, m, rows(half * HALF + at * BAND + part, BAND // 2), :].astype(F32)
                passed[c, m, half, side] = (mine + passing[c, m, half, side].astype(F32)).astype(BF16)
                send(("near", c, m, half), passed.at[c, m, half, side],
                     got1.at[c, m, half, side, pl.ds(part, BAND // 2)], peer)

    def rs_middle(c, m):
        for half, mine, _, peers in firsts:
            received(("near", c, m, half))
            total = (snd[c, m, rows(half * HALF + mine * BAND, BAND), :].astype(F32)
                     + got1[c, m, half, 0].astype(F32) + got1[c, m, half, 1].astype(F32))
            mid[c, m, half] = total.astype(BF16)
            for d, (peer, at) in enumerate(peers):
                send(("rs2", c, m, half), mid.at[c, m, half, rows(at * OWN, OWN)], got2.at[c, m, half, d], peer)

    def rs_end(c, m):
        parts = []
        for half, mine in ((0, y), (1, x)):
            received(("rs2", c, m, half))
            total = mid[c, m, half, rows(mine * OWN, OWN), :].astype(F32)
            for d in range(SIDE - 1):
                total = total + got2[c, m, half, d].astype(F32)
            parts.append(total)
        return jnp.concatenate(parts, axis=0)

    own_rows = (x * BAND + y * OWN, HALF + y * BAND + x * OWN)

    def ag_start(c, m, value):
        for half, _, _, peers in firsts:
            whole[c, m, rows(own_rows[half], OWN), :] = value[half * OWN:(half + 1) * OWN]
            for peer, _ in peers:
                place = whole.at[c, m, rows(own_rows[half], OWN)]
                send(("ag1", c, m, half), place, place, peer)

    def ag_middle(c, m):
        for half, mine, peers, _ in firsts:
            received(("ag1", c, m, half))
            (right, _), _, (left, _) = ring(peers)
            for peer, side, part in ((right, 0, UPPER), (left, 1, LOWER), (right, 0, LOWER), (left, 1, UPPER)):
                place = whole.at[c, m, rows(half * HALF + mine * BAND + part, BAND // 2)]
                early = (side, part) in ((0, UPPER), (1, LOWER))
                send(("ag2", c, m, half, side) if early else ("ag3", c, m, half), place, place, peer)

    def ag_relay(c, m):
        for half, _, peers, _ in firsts:
            (right, at_right), _, (left, at_left) = ring(peers)
            for side, peer, at, part in ((0, right, at_left, UPPER), (1, left, at_right, LOWER)):
                received(("ag2", c, m, half, side))
                place = whole.at[c, m, rows(half * HALF + at * BAND + part, BAND // 2)]
                send(("ag3", c, m, half), place, place, peer)

    def ag_end(c, m):
        for half in (0, 1):
            received(("ag3", c, m, half))

    def by_chunk(step):
        def body(i, carry):
            step(rows(i * CHUNK, CHUNK))
            return carry

        lax.fori_loop(0, TOK // CHUNK, body, 0)

    def forward_inner(b):
        a_in[b] = nn(k[b], w[b, 0])
        b_in[b] = nn(k[b], w[b, 2])

    def forward_target(b):
        step = jnp.broadcast_to(s[b], (128, TOK)).T
        for j in range(DIM // 128):
            lanes = slice(j * 128, (j + 1) * 128)
            target[b, :, lanes] = (step * v[b, :, lanes].astype(F32)).astype(BF16)

    def gate_step(gate, lift):
        sg = jax.nn.sigmoid(gate)
        activated = gate * sg
        return activated, lift * (sg * (1.0 + gate * (1.0 - sg)))

    def forward_rest(b):
        back[b] = nt(target[b], w[b, 1])

        def step(r):
            lift, hidden = b_in[b, r, :], back[b, r, :]
            activated, sloped = gate_step(a_in[b, r, :], lift)
            gated[b, r, :] = (activated * lift).astype(BF16)
            ga[b, r, :] = (hidden * sloped).astype(BF16)
            gb[b, r, :] = (hidden * activated).astype(BF16)

        by_chunk(step)

    def update_factors(b):
        def step(r):
            gate, lift, hidden = a_in[b, r, :], b_in[b, r, :], back[b, r, :]
            sg = jax.nn.sigmoid(gate)
            rest = 1.0 - sg
            slope = sg * (1.0 + gate * rest)
            curve = sg * rest * (2.0 + gate * (1.0 - 2.0 * sg))
            factors[0, r, :] = gate * sg
            factors[1, r, :] = lift * slope
            factors[2, r, :] = hidden * slope
            factors[3, r, :] = hidden * lift * curve

        by_chunk(step)

    def update_term(b, m):
        if m == 0:
            return tn(ga[b], k[b])
        if m == 1:
            return tn(target[b], gated[b])
        return tn(gb[b], k[b])

    row_of = lax.broadcasted_iota(jnp.int32, (2 * OWN, DIM), 0)
    col_of = lax.broadcasted_iota(jnp.int32, (2 * OWN, DIM), 1)
    wanted = jnp.where(row_of < OWN, own_rows[0] + row_of, own_rows[1] + row_of - OWN)
    picker = jnp.where(col_of == wanted, 1.0, 0.0).astype(BF16)

    def own_columns(b, m):
        mine = nt(picker, w[b, m])
        own_w[b, m] = mine
        kept[b, m] = jnp.broadcast_to(jnp.sqrt(jnp.sum(mine * mine, axis=1, keepdims=True) + EPSILON), (2 * OWN, 128))

    def own_update(b, m, change):
        total = own_w[b, m] + change
        own_p[b, m] = total
        summed[b, m] = jnp.broadcast_to(jnp.sqrt(jnp.sum(total * total, axis=1, keepdims=True) + EPSILON), (2 * OWN, 128))
        return total * (kept[b, m, :, :1] / summed[b, m, :, :1])

    def renorm_back(b, m, cotangent):
        matrix, before, after = own_p[b, m], kept[b, m, :, :1], summed[b, m, :, :1]
        inner = jnp.sum(cotangent * matrix, axis=1, keepdims=True)
        factor = before / after
        move = cotangent * factor - matrix * (factor * inner / (after * after))
        return move, own_w[b, m] * (inner / (after * before))

    def output_first():
        def step(r):
            lift = b_out[r, :]
            activated, sloped = gate_step(a_out[r, :], lift)
            gated_out[r, :] = (activated * lift).astype(BF16)
            a_out[r, :] = activated
            b_out[r, :] = sloped

        by_chunk(step)

    def output_second():
        def step(r):
            hidden = back_out[r, :]
            ga_out[r, :] = (hidden * b_out[r, :]).astype(BF16)
            gb_out[r, :] = (hidden * a_out[r, :]).astype(BF16)

        by_chunk(step)

    def store_out(i, b, value):
        for j in range(DIM // 128):
            out[i, pl.ds(b * TOK * 4 + j, TOK, stride=4), :] = value[:, j * 128:(j + 1) * 128]
        place = pl.ds(b * TOK * 4, TOK * 4)
        target_any = (query_any, key_any, value_any)[i]
        copy = pltpu.make_async_copy(out.at[i, place], target_any.at[place], out_sem.at[i, b])
        copy.start()
        return copy

    stores = []

    def hidden_step():
        def step(r):
            hidden_back[r, :] = (first_back[r, :] * factors[1, r, :] + third_back[r, :] * factors[0, r, :]).astype(BF16)

        by_chunk(step)

    def lift_step():
        def step(r):
            lift_back[r, :] = (first_back[r, :] * factors[2, r, :] + gated_back[r, :] * factors[0, r, :]).astype(BF16)

        by_chunk(step)

    def gate_backward():
        def step(r):
            gate_back[r, :] = (gated_back[r, :] * factors[1, r, :] + third_back[r, :] * factors[2, r, :]
                               + first_back[r, :] * factors[3, r, :]).astype(BF16)

        by_chunk(step)

    def update_inner(b, c, m):
        if m == 0:
            first_back[...] = nt(k[b], whole[c, 0])
        elif m == 1:
            gated_back[...] = nn(target[b], whole[c, 1])
        else:
            third_back[...] = nt(k[b], whole[c, 2])

    def scaled(b, total):
        step = jnp.broadcast_to(s[b], (128, TOK)).T
        return jnp.concatenate([total[:, j * 128:(j + 1) * 128] * step for j in range(DIM // 128)], axis=1)

    def start_term(m):
        if m == 0:
            return tn(gate_back[...], k[1])
        if m == 1:
            return tn(target[1], hidden_back[...])
        return tn(lift_back[...], k[1])

    def each(action, c, order):
        for m in order:
            action(c, m)

    order = (0, 2, 1)
    arrived(("k", 1), ("w", 1, 0), ("w", 1, 2))
    forward_inner(1)
    arrived("s", ("v", 1), ("w", 1, 1))
    forward_target(1)
    forward_rest(1)
    pl.semaphore_wait(barrier, 2 * (SIDE - 1))
    for m in (0, 2, 1):
        snd[D_LATE, m] = update_term(1, m).astype(BF16)
        rs_start(D_LATE, m)
    for m in (0, 2, 1):
        own_columns(1, m)
    arrived(("k", 0), ("w", 0, 0), ("w", 0, 2))
    forward_inner(0)
    rs_relay(D_LATE, 0)
    arrived(("v", 0), ("w", 0, 1))
    forward_target(0)
    rs_relay(D_LATE, 2)
    forward_rest(0)
    rs_relay(D_LATE, 1)
    each(rs_middle, D_LATE, (0, 2, 1))
    snd[D_EARLY, 0] = update_term(0, 0).astype(BF16)
    rs_start(D_EARLY, 0)
    snd[D_EARLY, 2] = update_term(0, 2).astype(BF16)
    for m in (0, 2, 1):
        renormed = own_update(1, m, rs_end(D_LATE, m))
        ag_start(R_LATE, m, renormed.astype(BF16))
    rs_start(D_EARLY, 2)
    snd[D_EARLY, 1] = update_term(0, 1).astype(BF16)
    arrived(("q", 0), ("g", 0))
    a_out[...] = nn(q[0], w[1, 0])
    b_out[...] = nn(q[0], w[1, 2])
    each(ag_middle, R_LATE, (0, 2, 1))
    back_out[...] = nt(g[0], w[1, 1])
    output_first()
    ag_relay(R_LATE, 0)
    output_second()
    ag_relay(R_LATE, 2)
    c_early[0] = tn(ga_out[...], q[0])
    ag_relay(R_LATE, 1)
    c_early[1] = tn(g[0], gated_out[...])
    c_early[2] = tn(gb_out[...], q[0])
    stores.append(store_out(0, 0, nt(ga_out[...], w[1, 0]) + nt(gb_out[...], w[1, 2])))
    for m in (0, 2, 1):
        own_columns(0, m)
    arrived(("q", 1), ("g", 1))
    ag_end(R_LATE, 0)
    a_out[...] = nt(q[1], whole[R_LATE, 0])
    ag_end(R_LATE, 2)
    b_out[...] = nt(q[1], whole[R_LATE, 2])
    output_first()
    snd[C_LATE, 1] = tn(g[1], gated_out[...]).astype(BF16)
    rs_start(C_LATE, 1)
    ag_end(R_LATE, 1)
    back_out[...] = nn(g[1], whole[R_LATE, 1])
    output_second()
    snd[C_LATE, 0] = tn(ga_out[...], q[1]).astype(BF16)
    rs_start(C_LATE, 0)
    snd[C_LATE, 2] = tn(gb_out[...], q[1]).astype(BF16)
    rs_start(C_LATE, 2)
    each(rs_relay, C_LATE, (1, 0, 2))
    rs_start(D_EARLY, 1)
    rs_relay(D_EARLY, 0)
    rs_relay(D_EARLY, 2)
    each(rs_middle, C_LATE, (1, 0, 2))
    stores.append(store_out(0, 1, nn(ga_out[...], whole[R_LATE, 0]) + nn(gb_out[...], whole[R_LATE, 2])))
    for m in (1, 0, 2):
        move, direct = renorm_back(1, m, rs_end(C_LATE, m))
        own_add[m] = move + direct
        ag_start(M_LATE, m, move.astype(BF16))
    update_factors(1)
    each(ag_middle, M_LATE, (1, 0, 2))
    rs_middle(D_EARLY, 0)
    rs_middle(D_EARLY, 2)
    rs_relay(D_EARLY, 1)
    each(ag_relay, M_LATE, (1, 0, 2))
    ag_end(M_LATE, 1)
    gated_back[...] = nn(target[1], whole[M_LATE, 1])
    ag_end(M_LATE, 0)
    first_back[...] = nt(k[1], whole[M_LATE, 0])
    lift_step()
    snd[C_EARLY, 2] = (c_early[2] + start_term(2)).astype(BF16)
    rs_start(C_EARLY, 2)
    ag_end(M_LATE, 2)
    third_back[...] = nt(k[1], whole[M_LATE, 2])
    gate_backward()
    snd[C_EARLY, 0] = (c_early[0] + start_term(0)).astype(BF16)
    rs_start(C_EARLY, 0)
    hidden_step()
    snd[C_EARLY, 1] = (c_early[1] + start_term(1)).astype(BF16)
    rs_start(C_EARLY, 1)
    each(rs_relay, C_EARLY, (2, 0, 1))
    rs_middle(D_EARLY, 1)
    each(rs_middle, C_EARLY, (2, 0, 1))
    stores.append(store_out(1, 1, nn(ga[1], whole[M_LATE, 0]) + nn(gb[1], whole[M_LATE, 2])
                            + nt(gate_back[...], w[1, 0]) + nt(lift_back[...], w[1, 2])))
    for m in (0, 2, 1):
        own_update(0, m, rs_end(D_EARLY, m))
    for m in (2, 0, 1):
        move, _ = renorm_back(0, m, rs_end(C_EARLY, m) + own_add[m])
        ag_start(M_EARLY, m, move.astype(BF16))
    stores.append(store_out(2, 1, scaled(1, nt(gated[1], whole[M_LATE, 1]) + nn(hidden_back[...], w[1, 1]))))
    each(ag_middle, M_EARLY, (2, 0, 1))
    update_factors(0)
    each(ag_relay, M_EARLY, (2, 0, 1))
    ag_end(M_EARLY, 2)
    third_back[...] = nt(k[0], whole[M_EARLY, 2])
    ag_end(M_EARLY, 0)
    first_back[...] = nt(k[0], whole[M_EARLY, 0])
    hidden_step()
    key_part = nn(ga[0], whole[M_EARLY, 0]) + nn(gb[0], whole[M_EARLY, 2])
    value_part = nn(hidden_back[...], w[0, 1])
    ag_end(M_EARLY, 1)
    gated_back[...] = nn(target[0], whole[M_EARLY, 1])
    lift_step()
    gate_backward()
    stores.append(store_out(1, 0, key_part + nt(gate_back[...], w[0, 0]) + nt(lift_back[...], w[0, 2])))
    stores.append(store_out(2, 0, scaled(0, value_part + nt(gated[0], whole[M_EARLY, 1]))))
    for copies in started.values():
        for copy in copies:
            copy.wait_send()
    for copy in stores:
        copy.wait()


def hand_out(query_any, key_any, value_any, query_out, key_out, value_out, held, in_sem, out_sem):
    size = held.shape[1] // PARTS
    pairs = ((query_any, query_out), (key_any, key_out), (value_any, value_out))
    loads, stores = [], []
    for i, (source, place) in enumerate(pairs):
        for j in range(PARTS):
            part = pl.ds(j * size, size)
            loads.append(pltpu.make_async_copy(source.at[part], held.at[i, part], in_sem.at[i, j]))
            stores.append(pltpu.make_async_copy(held.at[i, part], place.at[part], out_sem.at[i, j]))
    for copy in loads:
        copy.start()
    for load, store in zip(loads, stores):
        load.wait()
        store.start()
    for copy in stores:
        copy.wait()


def local(queries, key_rows, value_rows, step_sizes, out_grads, first_saved, second_saved, third_saved):
    vectors = [a.reshape(2, TOK, DIM) for a in (queries, key_rows, value_rows)]
    matrices = [a.reshape(2, DIM, DIM) for a in (first_saved, second_saved, third_saved)]
    anywhere = pl.BlockSpec(memory_space=pl.ANY)

    def vmem(*shape, dtype=F32):
        return pltpu.VMEM(shape, dtype)

    sem = pltpu.SemaphoreType.DMA
    result = pl.pallas_call(
        kernel,
        out_shape=[jax.ShapeDtypeStruct((2 * TOK * DIM // 128, 128), F32)] * 3,
        in_specs=[anywhere] * 8,
        out_specs=[anywhere] * 3,
        scratch_shapes=[
            vmem(2, TOK, DIM, dtype=BF16), vmem(2, TOK, DIM, dtype=BF16), vmem(2, TOK, DIM, dtype=BF16),
            vmem(2, 1, TOK), vmem(2, TOK, DIM, dtype=BF16), vmem(2, 3, DIM, DIM, dtype=BF16),
            *[vmem(2, TOK, DIM)] * 3, vmem(4, TOK, DIM),
            *[vmem(2, TOK, DIM, dtype=BF16)] * 4,
            *[vmem(TOK, DIM)] * 3,
            *[vmem(TOK, DIM, dtype=BF16)] * 3,
            *[vmem(TOK, DIM)] * 3,
            *[vmem(TOK, DIM, dtype=BF16)] * 3,
            vmem(3, DIM, DIM),
            vmem(2, 3, 2 * OWN, DIM), vmem(2, 3, 2 * OWN, DIM), vmem(3, 2 * OWN, DIM),
            vmem(2, 3, 2 * OWN, 128), vmem(2, 3, 2 * OWN, 128),
            vmem(4, 3, DIM, DIM, dtype=BF16),
            vmem(4, 3, 2, 2, BAND // 2, DIM, dtype=BF16),
            vmem(4, 3, 2, 2, BAND // 2, DIM, dtype=BF16),
            vmem(4, 3, 2, 2, BAND, DIM, dtype=BF16),
            vmem(4, 3, 2, BAND, DIM, dtype=BF16),
            vmem(4, 3, 2, SIDE - 1, OWN, DIM, dtype=BF16),
            vmem(3, 3, DIM, DIM, dtype=BF16),
            vmem(3, 2 * TOK * DIM // 128, 128),
            sem((17,)), sem((3, 2)), sem((378,)), sem((378,)),
        ],
        compiler_params=pltpu.CompilerParams(
            collective_id=0, has_side_effects=True, vmem_limit_bytes=60 * 2**20
        ),
        cost_estimate=pl.CostEstimate(flops=7 * 10**9, bytes_accessed=9 * 10**6, transcendentals=10**6),
    )(*vectors, step_sizes.reshape(2, 1, TOK), out_grads.reshape(2, TOK, DIM), *matrices)
    result = pl.pallas_call(
        hand_out,
        out_shape=[jax.ShapeDtypeStruct((2 * TOK * DIM // 128, 128), F32)] * 3,
        in_specs=[anywhere] * 3,
        out_specs=[anywhere] * 3,
        scratch_shapes=[vmem(3, 2 * TOK * DIM // 128, 128), sem((3, PARTS)), sem((3, PARTS))],
        cost_estimate=pl.CostEstimate(flops=0, bytes_accessed=6 * 10**6, transcendentals=0),
    )(*result)
    return tuple(part.reshape(2, TOK, 1, DIM) for part in result)


def solution(mesh):
    vectors, steps, matrices = P(None, "tok", "head", None), P(None, "tok", "head"), P(None, "head", None, None)
    return jax.shard_map(
        local,
        mesh=mesh,
        in_specs=(vectors, vectors, vectors, steps, vectors, matrices, matrices, matrices),
        out_specs=(vectors, vectors, vectors),
        check_vma=False,
    )
```

```python
import functools

import jax
import jax.numpy as jnp
from jax import lax
from jax.experimental import pallas as pl
from jax.experimental.pallas import tpu as pltpu
from jax.sharding import PartitionSpec as P

EPSILON = 1e-06
MESH = pl.DeviceIdType.MESH
F32, BF16 = jnp.float32, jnp.bfloat16
SIDE = 4
TOK, DIM = 256, 512
HALF = DIM // 2
BAND = HALF // SIDE
OWN = BAND // SIDE
PARTS = 4
CHUNK = 16
D_LATE, C_LATE, C_EARLY, D_EARLY = range(4)
R_LATE, M_LATE, M_EARLY = range(3)


def nn(left, right):
    return lax.dot_general(left, right, (((1,), (0,)), ((), ())), preferred_element_type=F32)


def nt(left, right):
    return lax.dot_general(left, right, (((1,), (1,)), ((), ())), preferred_element_type=F32)


def tn(left, right):
    return lax.dot_general(left, right, (((0,), (0,)), ((), ())), preferred_element_type=F32)


def kernel(
    q_any, k_any, v_any, s_any, g_any, w1_any, w2_any, w3_any,
    query_out, key_out, value_out,
    q, k, v, s, g, w,
    a_in, b_in, back, factors, gated, target, ga, gb,
    a_out, b_out, back_out, gated_out, ga_out, gb_out, ga_early, gb_early,
    first_back, third_back, gated_back, gate_back, hidden_back, lift_back,
    c_early, own_w, own_p, own_add, kept, summed,
    snd, passing, passed, got1, mid, got2, whole,
    in_sem, send_sem, recv_sem,
):
    tok = lax.axis_index("tok")
    x, y = lax.rem(tok, SIDE), tok // SIDE
    along_x = [(y * SIDE + lax.rem(x + d, SIDE), lax.rem(x + d, SIDE)) for d in range(1, SIDE)]
    along_y = [(lax.rem(y + d, SIDE) * SIDE + x, lax.rem(y + d, SIDE)) for d in range(1, SIDE)]

    weights_any = (w1_any, w2_any, w3_any)
    loads = {}

    def load(name, source, place):
        copy = pltpu.make_async_copy(source, place, in_sem.at[len(loads)])
        copy.start()
        loads[name] = copy

    def arrived(*names):
        for name in names:
            loads[name].wait()

    load("s", s_any, s)
    for b in (1, 0):
        load(("k", b), k_any.at[b], k.at[b])
        load(("w", b, 0), weights_any[0].at[b], w.at[b, 0])
        load(("w", b, 2), weights_any[2].at[b], w.at[b, 2])
        load(("v", b), v_any.at[b], v.at[b])
        load(("w", b, 1), weights_any[1].at[b], w.at[b, 1])
    for b in (0, 1):
        load(("q", b), q_any.at[b], q.at[b])
        load(("g", b), g_any.at[b], g.at[b])

    barrier = pltpu.get_barrier_semaphore()
    for peer, _ in along_x + along_y:
        pl.semaphore_signal(barrier, inc=1, device_id={"tok": peer}, device_id_type=MESH)

    started = {}
    sem_count = [0]

    def send(name, source, place, peer):
        n = sem_count[0]
        sem_count[0] = n + 1
        copy = pltpu.make_async_remote_copy(
            src_ref=source, dst_ref=place, send_sem=send_sem.at[n], recv_sem=recv_sem.at[n],
            device_id={"tok": peer}, device_id_type=MESH,
        )
        copy.start()
        started.setdefault(name, []).append(copy)

    def received(name):
        for copy in started[name]:
            copy.wait_recv()

    def rows(start, size):
        return pl.ds(pl.multiple_of(start, OWN), size)

    def ring(peers):
        return peers[0], peers[1], peers[2]

    firsts = ((0, x, along_x, along_y), (1, y, along_y, along_x))
    UPPER, LOWER = 0, BAND // 2

    def rs_start(c, m):
        for half, _, peers, _ in firsts:
            (right, at_right), (_, at_far), (left, at_left) = ring(peers)
            far, near_right, near_left = (half * HALF + at * BAND for at in (at_far, at_right, at_left))
            send(("far", c, m, half, 0), snd.at[c, m, rows(far + UPPER, BAND // 2)], passing.at[c, m, half, 0], right)
            send(("far", c, m, half, 1), snd.at[c, m, rows(far + LOWER, BAND // 2)], passing.at[c, m, half, 1], left)
            send(("near", c, m, half), snd.at[c, m, rows(near_right + LOWER, BAND // 2)],
                 got1.at[c, m, half, 0, pl.ds(LOWER, BAND // 2)], right)
            send(("near", c, m, half), snd.at[c, m, rows(near_left + UPPER, BAND // 2)],
                 got1.at[c, m, half, 1, pl.ds(UPPER, BAND // 2)], left)

    def rs_relay(c, m):
        for half, _, peers, _ in firsts:
            (right, at_right), _, (left, at_left) = ring(peers)
            for side, peer, at, part in ((0, right, at_right, UPPER), (1, left, at_left, LOWER)):
                received(("far", c, m, half, side))
                mine = snd[c, m, rows(half * HALF + at * BAND + part, BAND // 2), :].astype(F32)
                passed[c, m, half, side] = (mine + passing[c, m, half, side].astype(F32)).astype(BF16)
                send(("near", c, m, half), passed.at[c, m, half, side],
                     got1.at[c, m, half, side, pl.ds(part, BAND // 2)], peer)

    def rs_middle(c, m):
        for half, mine, _, peers in firsts:
            received(("near", c, m, half))
            total = (snd[c, m, rows(half * HALF + mine * BAND, BAND), :].astype(F32)
                     + got1[c, m, half, 0].astype(F32) + got1[c, m, half, 1].astype(F32))
            mid[c, m, half] = total.astype(BF16)
            for d, (peer, at) in enumerate(peers):
                send(("rs2", c, m, half), mid.at[c, m, half, rows(at * OWN, OWN)], got2.at[c, m, half, d], peer)

    def rs_end(c, m):
        parts = []
        for half, mine in ((0, y), (1, x)):
            received(("rs2", c, m, half))
            total = mid[c, m, half, rows(mine * OWN, OWN), :].astype(F32)
            for d in range(SIDE - 1):
                total = total + got2[c, m, half, d].astype(F32)
            parts.append(total)
        return jnp.concatenate(parts, axis=0)

    own_rows = (x * BAND + y * OWN, HALF + y * BAND + x * OWN)

    def ag_start(c, m, value):
        for half, _, _, peers in firsts:
            whole[c, m, rows(own_rows[half], OWN), :] = value[half * OWN:(half + 1) * OWN]
            for peer, _ in peers:
                place = whole.at[c, m, rows(own_rows[half], OWN)]
                send(("ag1", c, m, half), place, place, peer)

    def ag_middle(c, m):
        for half, mine, peers, _ in firsts:
            received(("ag1", c, m, half))
            (right, _), _, (left, _) = ring(peers)
            for peer, side, part in ((right, 0, UPPER), (left, 1, LOWER), (right, 0, LOWER), (left, 1, UPPER)):
                place = whole.at[c, m, rows(half * HALF + mine * BAND + part, BAND // 2)]
                early = (side, part) in ((0, UPPER), (1, LOWER))
                send(("ag2", c, m, half, side) if early else ("ag3", c, m, half), place, place, peer)

    def ag_relay(c, m):
        for half, _, peers, _ in firsts:
            (right, at_right), _, (left, at_left) = ring(peers)
            for side, peer, at, part in ((0, right, at_left, UPPER), (1, left, at_right, LOWER)):
                received(("ag2", c, m, half, side))
                place = whole.at[c, m, rows(half * HALF + at * BAND + part, BAND // 2)]
                send(("ag3", c, m, half), place, place, peer)

    def ag_end(c, m):
        for half in (0, 1):
            received(("ag3", c, m, half))

    def by_chunk(step):
        def body(i, carry):
            step(rows(i * CHUNK, CHUNK))
            return carry

        lax.fori_loop(0, TOK // CHUNK, body, 0, unroll=2)

    def forward_inner(b):
        a_in[b] = nn(k[b], w[b, 0])
        b_in[b] = nn(k[b], w[b, 2])

    def forward_target(b):
        step = jnp.broadcast_to(s[b], (128, TOK)).T
        for j in range(DIM // 128):
            lanes = slice(j * 128, (j + 1) * 128)
            target[b, :, lanes] = (step * v[b, :, lanes].astype(F32)).astype(BF16)

    def gate_step(gate, lift):
        sg = jax.nn.sigmoid(gate)
        activated = gate * sg
        return activated, lift * (sg * (1.0 + gate * (1.0 - sg)))

    def forward_rest(b):
        back[b] = nt(target[b], w[b, 1])

        def step(r):
            lift, hidden = b_in[b, r, :], back[b, r, :]
            activated, sloped = gate_step(a_in[b, r, :], lift)
            gated[b, r, :] = (activated * lift).astype(BF16)
            ga[b, r, :] = (hidden * sloped).astype(BF16)
            gb[b, r, :] = (hidden * activated).astype(BF16)

        by_chunk(step)

    def update_factors(b):
        def step(r):
            gate, lift, hidden = a_in[b, r, :], b_in[b, r, :], back[b, r, :]
            sg = jax.nn.sigmoid(gate)
            rest = 1.0 - sg
            slope = sg * (1.0 + gate * rest)
            curve = sg * rest * (2.0 + gate * (1.0 - 2.0 * sg))
            factors[0, r, :] = gate * sg
            factors[1, r, :] = lift * slope
            factors[2, r, :] = hidden * slope
            factors[3, r, :] = hidden * lift * curve

        by_chunk(step)

    def update_term(b, m):
        if m == 0:
            return tn(ga[b], k[b])
        if m == 1:
            return tn(target[b], gated[b])
        return tn(gb[b], k[b])

    row_of = lax.broadcasted_iota(jnp.int32, (2 * OWN, DIM), 0)
    col_of = lax.broadcasted_iota(jnp.int32, (2 * OWN, DIM), 1)
    wanted = jnp.where(row_of < OWN, own_rows[0] + row_of, own_rows[1] + row_of - OWN)
    picker = jnp.where(col_of == wanted, 1.0, 0.0).astype(BF16)

    def own_columns(b, m):
        mine = nt(picker, w[b, m])
        own_w[b, m] = mine
        kept[b, m] = jnp.broadcast_to(jnp.sqrt(jnp.sum(mine * mine, axis=1, keepdims=True) + EPSILON), (2 * OWN, 128))

    def own_update(b, m, change):
        total = own_w[b, m] + change
        own_p[b, m] = total
        summed[b, m] = jnp.broadcast_to(jnp.sqrt(jnp.sum(total * total, axis=1, keepdims=True) + EPSILON), (2 * OWN, 128))
        return total * (kept[b, m, :, :1] / summed[b, m, :, :1])

    def renorm_back(b, m, cotangent):
        matrix, before, after = own_p[b, m], kept[b, m, :, :1], summed[b, m, :, :1]
        inner = jnp.sum(cotangent * matrix, axis=1, keepdims=True)
        factor = before / after
        move = cotangent * factor - matrix * (factor * inner / (after * after))
        return move, own_w[b, m] * (inner / (after * before))

    def output_first():
        def step(r):
            lift = b_out[r, :]
            activated, sloped = gate_step(a_out[r, :], lift)
            gated_out[r, :] = (activated * lift).astype(BF16)
            a_out[r, :] = activated
            b_out[r, :] = sloped

        by_chunk(step)

    def output_second(ga_place, gb_place):
        def step(r):
            hidden = back_out[r, :]
            ga_place[r, :] = (hidden * b_out[r, :]).astype(BF16)
            gb_place[r, :] = (hidden * a_out[r, :]).astype(BF16)

        by_chunk(step)

    def store_out(i, b, value):
        place = (query_out, key_out, value_out)[i]
        for j in range(DIM // 128):
            place[pl.ds(b * TOK * 4 + j, TOK, stride=4), :] = value[:, j * 128:(j + 1) * 128]

    def hidden_step():
        def step(r):
            hidden_back[r, :] = (first_back[r, :] * factors[1, r, :] + third_back[r, :] * factors[0, r, :]).astype(BF16)

        by_chunk(step)

    def lift_step():
        def step(r):
            lift_back[r, :] = (first_back[r, :] * factors[2, r, :] + gated_back[r, :] * factors[0, r, :]).astype(BF16)

        by_chunk(step)

    def gate_backward():
        def step(r):
            gate_back[r, :] = (gated_back[r, :] * factors[1, r, :] + third_back[r, :] * factors[2, r, :]
                               + first_back[r, :] * factors[3, r, :]).astype(BF16)

        by_chunk(step)

    def update_inner(b, c, m):
        if m == 0:
            first_back[...] = nt(k[b], whole[c, 0])
        elif m == 1:
            gated_back[...] = nn(target[b], whole[c, 1])
        else:
            third_back[...] = nt(k[b], whole[c, 2])

    def scaled(b, total):
        step = jnp.broadcast_to(s[b], (128, TOK)).T
        return jnp.concatenate([total[:, j * 128:(j + 1) * 128] * step for j in range(DIM // 128)], axis=1)

    def start_term(m):
        if m == 0:
            return tn(gate_back[...], k[1])
        if m == 1:
            return tn(target[1], hidden_back[...])
        return tn(lift_back[...], k[1])

    def each(action, c, order):
        for m in order:
            action(c, m)

    order = (0, 2, 1)
    arrived(("k", 1), ("w", 1, 0), ("w", 1, 2))
    forward_inner(1)
    arrived("s", ("v", 1), ("w", 1, 1))
    forward_target(1)
    forward_rest(1)
    pl.semaphore_wait(barrier, 2 * (SIDE - 1))
    for m in (0, 2, 1):
        snd[D_LATE, m] = update_term(1, m).astype(BF16)
        rs_start(D_LATE, m)
    for m in (0, 2, 1):
        own_columns(1, m)
    arrived(("k", 0), ("w", 0, 0), ("w", 0, 2))
    forward_inner(0)
    rs_relay(D_LATE, 0)
    arrived(("v", 0), ("w", 0, 1))
    forward_target(0)
    rs_relay(D_LATE, 2)
    forward_rest(0)
    rs_relay(D_LATE, 1)
    each(rs_middle, D_LATE, (0, 2, 1))
    snd[D_EARLY, 0] = update_term(0, 0).astype(BF16)
    rs_start(D_EARLY, 0)
    snd[D_EARLY, 2] = update_term(0, 2).astype(BF16)
    for m in (0, 2, 1):
        renormed = own_update(1, m, rs_end(D_LATE, m))
        ag_start(R_LATE, m, renormed.astype(BF16))
    rs_start(D_EARLY, 2)
    snd[D_EARLY, 1] = update_term(0, 1).astype(BF16)
    arrived(("q", 0), ("g", 0))
    a_out[...] = nn(q[0], w[1, 0])
    b_out[...] = nn(q[0], w[1, 2])
    each(ag_middle, R_LATE, (0, 2, 1))
    back_out[...] = nt(g[0], w[1, 1])
    output_first()
    ag_relay(R_LATE, 0)
    output_second(ga_early, gb_early)
    ag_relay(R_LATE, 2)
    c_early[0] = tn(ga_early[...], q[0])
    c_early[2] = tn(gb_early[...], q[0])
    ag_relay(R_LATE, 1)
    rs_start(D_EARLY, 1)
    rs_relay(D_EARLY, 0)
    rs_relay(D_EARLY, 2)
    c_early[1] = tn(g[0], gated_out[...])
    arrived(("q", 1), ("g", 1))
    ag_end(R_LATE, 0)
    a_out[...] = nt(q[1], whole[R_LATE, 0])
    ag_end(R_LATE, 2)
    b_out[...] = nt(q[1], whole[R_LATE, 2])
    output_first()
    snd[C_LATE, 1] = tn(g[1], gated_out[...]).astype(BF16)
    rs_start(C_LATE, 1)
    ag_end(R_LATE, 1)
    back_out[...] = nn(g[1], whole[R_LATE, 1])
    output_second(ga_out, gb_out)
    snd[C_LATE, 0] = tn(ga_out[...], q[1]).astype(BF16)
    rs_start(C_LATE, 0)
    snd[C_LATE, 2] = tn(gb_out[...], q[1]).astype(BF16)
    rs_start(C_LATE, 2)
    own_columns(0, 0)
    rs_relay(C_LATE, 1)
    own_columns(0, 2)
    rs_relay(C_LATE, 0)
    own_columns(0, 1)
    rs_relay(C_LATE, 2)
    each(rs_middle, C_LATE, (1, 0, 2))
    rs_relay(D_EARLY, 1)
    store_out(0, 1, nn(ga_out[...], whole[R_LATE, 0]) + nn(gb_out[...], whole[R_LATE, 2]))
    for m in (1, 0, 2):
        move, direct = renorm_back(1, m, rs_end(C_LATE, m))
        own_add[m] = move + direct
        ag_start(M_LATE, m, move.astype(BF16))
    rs_middle(D_EARLY, 0)
    rs_middle(D_EARLY, 2)
    update_factors(1)
    each(ag_middle, M_LATE, (1, 0, 2))
    store_out(0, 0, nt(ga_early[...], w[1, 0]) + nt(gb_early[...], w[1, 2]))
    each(ag_relay, M_LATE, (1, 0, 2))
    rs_middle(D_EARLY, 1)
    ag_end(M_LATE, 1)
    gated_back[...] = nn(target[1], whole[M_LATE, 1])
    ag_end(M_LATE, 0)
    first_back[...] = nt(k[1], whole[M_LATE, 0])
    lift_step()
    snd[C_EARLY, 2] = (c_early[2] + start_term(2)).astype(BF16)
    rs_start(C_EARLY, 2)
    ag_end(M_LATE, 2)
    third_back[...] = nt(k[1], whole[M_LATE, 2])
    gate_backward()
    snd[C_EARLY, 0] = (c_early[0] + start_term(0)).astype(BF16)
    rs_start(C_EARLY, 0)
    hidden_step()
    snd[C_EARLY, 1] = (c_early[1] + start_term(1)).astype(BF16)
    rs_start(C_EARLY, 1)
    each(rs_relay, C_EARLY, (2, 0, 1))
    each(rs_middle, C_EARLY, (2, 0, 1))
    store_out(1, 1, nn(ga[1], whole[M_LATE, 0]) + nn(gb[1], whole[M_LATE, 2])
              + nt(gate_back[...], w[1, 0]) + nt(lift_back[...], w[1, 2]))
    for m in (0, 2, 1):
        own_update(0, m, rs_end(D_EARLY, m))
    for m in (2, 0, 1):
        move, _ = renorm_back(0, m, rs_end(C_EARLY, m) + own_add[m])
        ag_start(M_EARLY, m, move.astype(BF16))
    store_out(2, 1, scaled(1, nt(gated[1], whole[M_LATE, 1]) + nn(hidden_back[...], w[1, 1])))
    each(ag_middle, M_EARLY, (2, 0, 1))
    update_factors(0)
    each(ag_relay, M_EARLY, (2, 0, 1))
    ag_end(M_EARLY, 2)
    third_back[...] = nt(k[0], whole[M_EARLY, 2])
    ag_end(M_EARLY, 0)
    first_back[...] = nt(k[0], whole[M_EARLY, 0])
    hidden_step()
    key_part = nn(ga[0], whole[M_EARLY, 0]) + nn(gb[0], whole[M_EARLY, 2])
    value_part = nn(hidden_back[...], w[0, 1])
    ag_end(M_EARLY, 1)
    gated_back[...] = nn(target[0], whole[M_EARLY, 1])
    lift_step()
    gate_backward()
    store_out(1, 0, key_part + nt(gate_back[...], w[0, 0]) + nt(lift_back[...], w[0, 2]))
    store_out(2, 0, scaled(0, value_part + nt(gated[0], whole[M_EARLY, 1])))
    for copies in started.values():
        for copy in copies:
            copy.wait_send()


def hand_out(query_ref, key_ref, value_ref, query_out, key_out, value_out, sems):
    pairs = ((query_ref, query_out), (key_ref, key_out), (value_ref, value_out))
    copies = []
    for i, (source, place) in enumerate(pairs):
        for j in range(PARTS):
            part = pl.ds(j * (source.shape[0] // PARTS), source.shape[0] // PARTS)
            copies.append(pltpu.make_async_copy(source.at[part], place.at[part], sems.at[i, j]))
    for copy in copies:
        copy.start()
    for copy in copies:
        copy.wait()


def local(queries, key_rows, value_rows, step_sizes, out_grads, first_saved, second_saved, third_saved):
    vectors = [a.reshape(2, TOK, DIM) for a in (queries, key_rows, value_rows)]
    matrices = [a.reshape(2, DIM, DIM) for a in (first_saved, second_saved, third_saved)]
    anywhere = pl.BlockSpec(memory_space=pl.ANY)

    def vmem(*shape, dtype=F32):
        return pltpu.VMEM(shape, dtype)

    sem = pltpu.SemaphoreType.DMA
    result = pl.pallas_call(
        kernel,
        out_shape=[vmem(2 * TOK * DIM // 128, 128)] * 3,
        in_specs=[anywhere] * 8,
        out_specs=[pl.BlockSpec(memory_space=pltpu.VMEM)] * 3,
        scratch_shapes=[
            vmem(2, TOK, DIM, dtype=BF16), vmem(2, TOK, DIM, dtype=BF16), vmem(2, TOK, DIM, dtype=BF16),
            vmem(2, 1, TOK), vmem(2, TOK, DIM, dtype=BF16), vmem(2, 3, DIM, DIM, dtype=BF16),
            *[vmem(2, TOK, DIM)] * 3, vmem(4, TOK, DIM),
            *[vmem(2, TOK, DIM, dtype=BF16)] * 4,
            *[vmem(TOK, DIM)] * 3,
            *[vmem(TOK, DIM, dtype=BF16)] * 5,
            *[vmem(TOK, DIM)] * 3,
            *[vmem(TOK, DIM, dtype=BF16)] * 3,
            vmem(3, DIM, DIM),
            vmem(2, 3, 2 * OWN, DIM), vmem(2, 3, 2 * OWN, DIM), vmem(3, 2 * OWN, DIM),
            vmem(2, 3, 2 * OWN, 128), vmem(2, 3, 2 * OWN, 128),
            vmem(4, 3, DIM, DIM, dtype=BF16),
            vmem(4, 3, 2, 2, BAND // 2, DIM, dtype=BF16),
            vmem(4, 3, 2, 2, BAND // 2, DIM, dtype=BF16),
            vmem(4, 3, 2, 2, BAND, DIM, dtype=BF16),
            vmem(4, 3, 2, BAND, DIM, dtype=BF16),
            vmem(4, 3, 2, SIDE - 1, OWN, DIM, dtype=BF16),
            vmem(3, 3, DIM, DIM, dtype=BF16),
            sem((17,)), sem((378,)), sem((378,)),
        ],
        compiler_params=pltpu.CompilerParams(
            collective_id=0, has_side_effects=True, vmem_limit_bytes=54 * 2**20
        ),
        cost_estimate=pl.CostEstimate(flops=7 * 10**9, bytes_accessed=9 * 10**6, transcendentals=10**6),
    )(*vectors, step_sizes.reshape(2, 1, TOK), out_grads.reshape(2, TOK, DIM), *matrices)
    result = pl.pallas_call(
        hand_out,
        out_shape=[jax.ShapeDtypeStruct((2 * TOK * DIM // 128, 128), F32)] * 3,
        in_specs=[pl.BlockSpec(memory_space=pltpu.VMEM)] * 3,
        out_specs=[anywhere] * 3,
        scratch_shapes=[sem((3, PARTS))],
        cost_estimate=pl.CostEstimate(flops=0, bytes_accessed=6 * 10**6, transcendentals=0),
    )(*[pltpu.with_memory_space_constraint(part, pltpu.VMEM) for part in result])
    return tuple(part.reshape(2, TOK, 1, DIM) for part in result)


def solution(mesh):
    vectors, steps, matrices = P(None, "tok", "head", None), P(None, "tok", "head"), P(None, "head", None, None)
    return jax.shard_map(
        local,
        mesh=mesh,
        in_specs=(vectors, vectors, vectors, steps, vectors, matrices, matrices, matrices),
        out_specs=(vectors, vectors, vectors),
        check_vma=False,
    )
```

```python
import functools

import jax
import jax.numpy as jnp
from jax import lax
from jax.experimental import pallas as pl
from jax.experimental.pallas import tpu as pltpu
from jax.sharding import PartitionSpec as P

EPSILON = 1e-06
MESH = pl.DeviceIdType.MESH
F32, BF16 = jnp.float32, jnp.bfloat16
SIDE = 4
TOK, DIM = 256, 512
HALF = DIM // 2
BAND = HALF // SIDE
OWN = BAND // SIDE
CHUNK = 16
D_LATE, C_LATE, C_EARLY, D_EARLY = range(4)
R_LATE, M_LATE, M_EARLY = range(3)


def nn(left, right):
    return lax.dot_general(left, right, (((1,), (0,)), ((), ())), preferred_element_type=F32)


def nt(left, right):
    return lax.dot_general(left, right, (((1,), (1,)), ((), ())), preferred_element_type=F32)


def tn(left, right):
    return lax.dot_general(left, right, (((0,), (0,)), ((), ())), preferred_element_type=F32)


def by_chunk(step):
    def body(i, carry):
        step(pl.ds(pl.multiple_of(i * CHUNK, CHUNK), CHUNK))
        return carry

    lax.fori_loop(0, TOK // CHUNK, body, 0, unroll=2)


def hidden_of(first_back, third_back, factors, r):
    return (first_back[r, :] * factors[1, r, :] + third_back[r, :] * factors[0, r, :]).astype(BF16)


def lift_of(first_back, gated_back, factors, r):
    return (first_back[r, :] * factors[2, r, :] + gated_back[r, :] * factors[0, r, :]).astype(BF16)


def gate_of(first_back, third_back, gated_back, factors, r):
    return (gated_back[r, :] * factors[1, r, :] + third_back[r, :] * factors[2, r, :]
            + first_back[r, :] * factors[3, r, :]).astype(BF16)


def spread(place, start, value):
    for j in range(DIM // 128):
        place[pl.ds(start * 4 + j, TOK, stride=4), :] = value[:, j * 128:(j + 1) * 128]


def scaled(steps, total):
    step = jnp.broadcast_to(steps, (128, TOK)).T
    return jnp.concatenate([total[:, j * 128:(j + 1) * 128] * step for j in range(DIM // 128)], axis=1)


def kernel(
    q_any, k_any, v_any, s_any, g_any, w1_any, w2_any, w3_any,
    query_out, key_out, value_out, key_part, value_part, first_back, third_back, gated_back, factors, w,
    q, k, v, s, g,
    a_in, b_in, back, gated, target, ga, gb,
    a_out, b_out, back_out, gated_out, ga_out, gb_out, ga_early, gb_early,
    gate_back, hidden_back, lift_back,
    c_early, own_w, own_p, own_add, kept, summed,
    snd, passing, passed, got1, mid, got2, whole,
    in_sem, send_sem, recv_sem,
):
    tok = lax.axis_index("tok")
    x, y = lax.rem(tok, SIDE), tok // SIDE
    along_x = [(y * SIDE + lax.rem(x + d, SIDE), lax.rem(x + d, SIDE)) for d in range(1, SIDE)]
    along_y = [(lax.rem(y + d, SIDE) * SIDE + x, lax.rem(y + d, SIDE)) for d in range(1, SIDE)]

    weights_any = (w1_any, w2_any, w3_any)
    loads = {}

    def load(name, source, place):
        copy = pltpu.make_async_copy(source, place, in_sem.at[len(loads)])
        copy.start()
        loads[name] = copy

    def arrived(*names):
        for name in names:
            loads[name].wait()

    load("s", s_any, s)
    for b in (1, 0):
        load(("k", b), k_any.at[b], k.at[b])
        load(("w", b, 0), weights_any[0].at[b], w.at[b, 0])
        load(("w", b, 2), weights_any[2].at[b], w.at[b, 2])
        load(("v", b), v_any.at[b], v.at[b])
        load(("w", b, 1), weights_any[1].at[b], w.at[b, 1])
    for b in (0, 1):
        load(("q", b), q_any.at[b], q.at[b])
        load(("g", b), g_any.at[b], g.at[b])

    barrier = pltpu.get_barrier_semaphore()
    for peer, _ in along_x + along_y:
        pl.semaphore_signal(barrier, inc=1, device_id={"tok": peer}, device_id_type=MESH)

    started = {}
    sem_count = [0]

    def send(name, source, place, peer):
        n = sem_count[0]
        sem_count[0] = n + 1
        copy = pltpu.make_async_remote_copy(
            src_ref=source, dst_ref=place, send_sem=send_sem.at[n], recv_sem=recv_sem.at[n],
            device_id={"tok": peer}, device_id_type=MESH,
        )
        copy.start()
        started.setdefault(name, []).append(copy)

    def received(name):
        for copy in started[name]:
            copy.wait_recv()

    def rows(start, size):
        return pl.ds(pl.multiple_of(start, OWN), size)

    def ring(peers):
        return peers[0], peers[1], peers[2]

    firsts = ((0, x, along_x, along_y), (1, y, along_y, along_x))
    UPPER, LOWER = 0, BAND // 2

    def rs_start(c, m):
        for half, _, peers, _ in firsts:
            (right, at_right), (_, at_far), (left, at_left) = ring(peers)
            far, near_right, near_left = (half * HALF + at * BAND for at in (at_far, at_right, at_left))
            send(("far", c, m, half, 0), snd.at[c, m, rows(far + UPPER, BAND // 2)], passing.at[c, m, half, 0], right)
            send(("far", c, m, half, 1), snd.at[c, m, rows(far + LOWER, BAND // 2)], passing.at[c, m, half, 1], left)
            send(("near", c, m, half), snd.at[c, m, rows(near_right + LOWER, BAND // 2)],
                 got1.at[c, m, half, 0, pl.ds(LOWER, BAND // 2)], right)
            send(("near", c, m, half), snd.at[c, m, rows(near_left + UPPER, BAND // 2)],
                 got1.at[c, m, half, 1, pl.ds(UPPER, BAND // 2)], left)

    def rs_relay(c, m):
        for half, _, peers, _ in firsts:
            (right, at_right), _, (left, at_left) = ring(peers)
            for side, peer, at, part in ((0, right, at_right, UPPER), (1, left, at_left, LOWER)):
                received(("far", c, m, half, side))
                mine = snd[c, m, rows(half * HALF + at * BAND + part, BAND // 2), :].astype(F32)
                passed[c, m, half, side] = (mine + passing[c, m, half, side].astype(F32)).astype(BF16)
                send(("near", c, m, half), passed.at[c, m, half, side],
                     got1.at[c, m, half, side, pl.ds(part, BAND // 2)], peer)

    def rs_middle(c, m):
        for half, mine, _, peers in firsts:
            received(("near", c, m, half))
            total = (snd[c, m, rows(half * HALF + mine * BAND, BAND), :].astype(F32)
                     + got1[c, m, half, 0].astype(F32) + got1[c, m, half, 1].astype(F32))
            mid[c, m, half] = total.astype(BF16)
            for d, (peer, at) in enumerate(peers):
                send(("rs2", c, m, half), mid.at[c, m, half, rows(at * OWN, OWN)], got2.at[c, m, half, d], peer)

    def rs_end(c, m):
        parts = []
        for half, mine in ((0, y), (1, x)):
            received(("rs2", c, m, half))
            total = mid[c, m, half, rows(mine * OWN, OWN), :].astype(F32)
            for d in range(SIDE - 1):
                total = total + got2[c, m, half, d].astype(F32)
            parts.append(total)
        return jnp.concatenate(parts, axis=0)

    own_rows = (x * BAND + y * OWN, HALF + y * BAND + x * OWN)

    def ag_start(c, m, value):
        for half, _, _, peers in firsts:
            whole[c, m, rows(own_rows[half], OWN), :] = value[half * OWN:(half + 1) * OWN]
            for peer, _ in peers:
                place = whole.at[c, m, rows(own_rows[half], OWN)]
                send(("ag1", c, m, half), place, place, peer)

    def ag_middle(c, m):
        for half, mine, peers, _ in firsts:
            received(("ag1", c, m, half))
            (right, _), _, (left, _) = ring(peers)
            for peer, side, part in ((right, 0, UPPER), (left, 1, LOWER), (right, 0, LOWER), (left, 1, UPPER)):
                place = whole.at[c, m, rows(half * HALF + mine * BAND + part, BAND // 2)]
                early = (side, part) in ((0, UPPER), (1, LOWER))
                send(("ag2", c, m, half, side) if early else ("ag3", c, m, half), place, place, peer)

    def ag_relay(c, m):
        for half, _, peers, _ in firsts:
            (right, at_right), _, (left, at_left) = ring(peers)
            for side, peer, at, part in ((0, right, at_left, UPPER), (1, left, at_right, LOWER)):
                received(("ag2", c, m, half, side))
                place = whole.at[c, m, rows(half * HALF + at * BAND + part, BAND // 2)]
                send(("ag3", c, m, half), place, place, peer)

    def ag_end(c, m):
        for half in (0, 1):
            received(("ag3", c, m, half))

    def forward_inner(b):
        a_in[b] = nn(k[b], w[b, 0])
        b_in[b] = nn(k[b], w[b, 2])

    def forward_target(b):
        step = jnp.broadcast_to(s[b], (128, TOK)).T
        for j in range(DIM // 128):
            lanes = slice(j * 128, (j + 1) * 128)
            target[b, :, lanes] = (step * v[b, :, lanes].astype(F32)).astype(BF16)

    def gate_step(gate, lift):
        sg = jax.nn.sigmoid(gate)
        activated = gate * sg
        return activated, lift * (sg * (1.0 + gate * (1.0 - sg)))

    def forward_rest(b):
        back[b] = nt(target[b], w[b, 1])

        def step(r):
            lift, hidden = b_in[b, r, :], back[b, r, :]
            activated, sloped = gate_step(a_in[b, r, :], lift)
            gated[b, r, :] = (activated * lift).astype(BF16)
            ga[b, r, :] = (hidden * sloped).astype(BF16)
            gb[b, r, :] = (hidden * activated).astype(BF16)

        by_chunk(step)

    def update_factors(b):
        def step(r):
            gate, lift, hidden = a_in[b, r, :], b_in[b, r, :], back[b, r, :]
            sg = jax.nn.sigmoid(gate)
            rest = 1.0 - sg
            slope = sg * (1.0 + gate * rest)
            curve = sg * rest * (2.0 + gate * (1.0 - 2.0 * sg))
            factors[0, r, :] = gate * sg
            factors[1, r, :] = lift * slope
            factors[2, r, :] = hidden * slope
            factors[3, r, :] = hidden * lift * curve

        by_chunk(step)

    def update_term(b, m):
        if m == 0:
            return tn(ga[b], k[b])
        if m == 1:
            return tn(target[b], gated[b])
        return tn(gb[b], k[b])

    row_of = lax.broadcasted_iota(jnp.int32, (2 * OWN, DIM), 0)
    col_of = lax.broadcasted_iota(jnp.int32, (2 * OWN, DIM), 1)
    wanted = jnp.where(row_of < OWN, own_rows[0] + row_of, own_rows[1] + row_of - OWN)
    picker = jnp.where(col_of == wanted, 1.0, 0.0).astype(BF16)

    def own_columns(b, m):
        mine = nt(picker, w[b, m])
        own_w[b, m] = mine
        kept[b, m] = jnp.broadcast_to(jnp.sqrt(jnp.sum(mine * mine, axis=1, keepdims=True) + EPSILON), (2 * OWN, 128))

    def own_update(b, m, change):
        total = own_w[b, m] + change
        own_p[b, m] = total
        summed[b, m] = jnp.broadcast_to(jnp.sqrt(jnp.sum(total * total, axis=1, keepdims=True) + EPSILON), (2 * OWN, 128))
        return total * (kept[b, m, :, :1] / summed[b, m, :, :1])

    def renorm_back(b, m, cotangent):
        matrix, before, after = own_p[b, m], kept[b, m, :, :1], summed[b, m, :, :1]
        inner = jnp.sum(cotangent * matrix, axis=1, keepdims=True)
        factor = before / after
        move = cotangent * factor - matrix * (factor * inner / (after * after))
        return move, own_w[b, m] * (inner / (after * before))

    def output_first():
        def step(r):
            lift = b_out[r, :]
            activated, sloped = gate_step(a_out[r, :], lift)
            gated_out[r, :] = (activated * lift).astype(BF16)
            a_out[r, :] = activated
            b_out[r, :] = sloped

        by_chunk(step)

    def output_second(ga_place, gb_place):
        def step(r):
            hidden = back_out[r, :]
            ga_place[r, :] = (hidden * b_out[r, :]).astype(BF16)
            gb_place[r, :] = (hidden * a_out[r, :]).astype(BF16)

        by_chunk(step)

    def hidden_step():
        def step(r):
            hidden_back[r, :] = hidden_of(first_back, third_back, factors, r)

        by_chunk(step)

    def lift_step():
        def step(r):
            lift_back[r, :] = lift_of(first_back, gated_back, factors, r)

        by_chunk(step)

    def gate_backward():
        def step(r):
            gate_back[r, :] = gate_of(first_back, third_back, gated_back, factors, r)

        by_chunk(step)

    def update_inner(b, c, m):
        if m == 0:
            first_back[...] = nt(k[b], whole[c, 0])
        elif m == 1:
            gated_back[...] = nn(target[b], whole[c, 1])
        else:
            third_back[...] = nt(k[b], whole[c, 2])

    def start_term(m):
        if m == 0:
            return tn(gate_back[...], k[1])
        if m == 1:
            return tn(target[1], hidden_back[...])
        return tn(lift_back[...], k[1])

    def each(action, c, order):
        for m in order:
            action(c, m)

    order = (0, 2, 1)
    arrived(("k", 1), ("w", 1, 0), ("w", 1, 2))
    forward_inner(1)
    arrived("s", ("v", 1), ("w", 1, 1))
    forward_target(1)
    forward_rest(1)
    pl.semaphore_wait(barrier, 2 * (SIDE - 1))
    for m in (0, 2, 1):
        snd[D_LATE, m] = update_term(1, m).astype(BF16)
        rs_start(D_LATE, m)
    for m in (0, 2, 1):
        own_columns(1, m)
    arrived(("k", 0), ("w", 0, 0), ("w", 0, 2))
    forward_inner(0)
    rs_relay(D_LATE, 0)
    arrived(("v", 0), ("w", 0, 1))
    forward_target(0)
    rs_relay(D_LATE, 2)
    forward_rest(0)
    rs_relay(D_LATE, 1)
    each(rs_middle, D_LATE, (0, 2, 1))
    snd[D_EARLY, 0] = update_term(0, 0).astype(BF16)
    rs_start(D_EARLY, 0)
    snd[D_EARLY, 2] = update_term(0, 2).astype(BF16)
    for m in (0, 2, 1):
        renormed = own_update(1, m, rs_end(D_LATE, m))
        ag_start(R_LATE, m, renormed.astype(BF16))
    rs_start(D_EARLY, 2)
    snd[D_EARLY, 1] = update_term(0, 1).astype(BF16)
    arrived(("q", 0), ("g", 0))
    a_out[...] = nn(q[0], w[1, 0])
    b_out[...] = nn(q[0], w[1, 2])
    each(ag_middle, R_LATE, (0, 2, 1))
    back_out[...] = nt(g[0], w[1, 1])
    output_first()
    ag_relay(R_LATE, 0)
    output_second(ga_early, gb_early)
    ag_relay(R_LATE, 2)
    c_early[0] = tn(ga_early[...], q[0])
    c_early[2] = tn(gb_early[...], q[0])
    ag_relay(R_LATE, 1)
    rs_start(D_EARLY, 1)
    rs_relay(D_EARLY, 0)
    rs_relay(D_EARLY, 2)
    c_early[1] = tn(g[0], gated_out[...])
    arrived(("q", 1), ("g", 1))
    ag_end(R_LATE, 0)
    a_out[...] = nt(q[1], whole[R_LATE, 0])
    ag_end(R_LATE, 2)
    b_out[...] = nt(q[1], whole[R_LATE, 2])
    output_first()
    snd[C_LATE, 1] = tn(g[1], gated_out[...]).astype(BF16)
    rs_start(C_LATE, 1)
    ag_end(R_LATE, 1)
    back_out[...] = nn(g[1], whole[R_LATE, 1])
    output_second(ga_out, gb_out)
    snd[C_LATE, 0] = tn(ga_out[...], q[1]).astype(BF16)
    rs_start(C_LATE, 0)
    snd[C_LATE, 2] = tn(gb_out[...], q[1]).astype(BF16)
    rs_start(C_LATE, 2)
    own_columns(0, 0)
    rs_relay(C_LATE, 1)
    own_columns(0, 2)
    rs_relay(C_LATE, 0)
    own_columns(0, 1)
    rs_relay(C_LATE, 2)
    each(rs_middle, C_LATE, (1, 0, 2))
    rs_relay(D_EARLY, 1)
    spread(query_out, TOK, nn(ga_out[...], whole[R_LATE, 0]) + nn(gb_out[...], whole[R_LATE, 2]))
    for m in (1, 0, 2):
        move, direct = renorm_back(1, m, rs_end(C_LATE, m))
        own_add[m] = move + direct
        ag_start(M_LATE, m, move.astype(BF16))
    rs_middle(D_EARLY, 0)
    rs_middle(D_EARLY, 2)
    update_factors(1)
    each(ag_middle, M_LATE, (1, 0, 2))
    spread(query_out, 0, nt(ga_early[...], w[1, 0]) + nt(gb_early[...], w[1, 2]))
    each(ag_relay, M_LATE, (1, 0, 2))
    rs_middle(D_EARLY, 1)
    ag_end(M_LATE, 1)
    gated_back[...] = nn(target[1], whole[M_LATE, 1])
    ag_end(M_LATE, 0)
    first_back[...] = nt(k[1], whole[M_LATE, 0])
    lift_step()
    snd[C_EARLY, 2] = (c_early[2] + start_term(2)).astype(BF16)
    rs_start(C_EARLY, 2)
    ag_end(M_LATE, 2)
    third_back[...] = nt(k[1], whole[M_LATE, 2])
    gate_backward()
    snd[C_EARLY, 0] = (c_early[0] + start_term(0)).astype(BF16)
    rs_start(C_EARLY, 0)
    hidden_step()
    snd[C_EARLY, 1] = (c_early[1] + start_term(1)).astype(BF16)
    rs_start(C_EARLY, 1)
    each(rs_relay, C_EARLY, (2, 0, 1))
    each(rs_middle, C_EARLY, (2, 0, 1))
    spread(key_out, 0, nn(ga[1], whole[M_LATE, 0]) + nn(gb[1], whole[M_LATE, 2])
           + nt(gate_back[...], w[1, 0]) + nt(lift_back[...], w[1, 2]))
    for m in (0, 2, 1):
        own_update(0, m, rs_end(D_EARLY, m))
    for m in (2, 0, 1):
        move, _ = renorm_back(0, m, rs_end(C_EARLY, m) + own_add[m])
        ag_start(M_EARLY, m, move.astype(BF16))
    spread(value_out, 0, scaled(s[1], nt(gated[1], whole[M_LATE, 1]) + nn(hidden_back[...], w[1, 1])))
    each(ag_middle, M_EARLY, (2, 0, 1))
    update_factors(0)
    each(ag_relay, M_EARLY, (2, 0, 1))
    ag_end(M_EARLY, 2)
    third_back[...] = nt(k[0], whole[M_EARLY, 2])
    ag_end(M_EARLY, 0)
    first_back[...] = nt(k[0], whole[M_EARLY, 0])
    key_part[...] = nn(ga[0], whole[M_EARLY, 0]) + nn(gb[0], whole[M_EARLY, 2])
    ag_end(M_EARLY, 1)
    gated_back[...] = nn(target[0], whole[M_EARLY, 1])
    value_part[...] = nt(gated[0], whole[M_EARLY, 1])
    for copies in started.values():
        for copy in copies:
            copy.wait_send()


def last_step(
    steps, query_ref, key_ref, value_ref, key_part, value_part, first_back, third_back, gated_back, factors, w,
    query_out, key_out, value_out,
    gate_back, hidden_back, lift_back, key_last, value_last, sems,
):
    lines = key_ref.shape[0]
    copies = []

    def leave(source, place):
        copy = pltpu.make_async_copy(source, place, sems.at[len(copies)])
        copy.start()
        copies.append(copy)

    first, second = pl.ds(0, lines), pl.ds(lines, lines)
    leave(query_ref.at[first], query_out.at[first])
    leave(query_ref.at[second], query_out.at[second])
    leave(key_ref, key_out.at[second])
    leave(value_ref, value_out.at[second])

    def step(r):
        hidden_back[r, :] = hidden_of(first_back, third_back, factors, r)
        lift_back[r, :] = lift_of(first_back, gated_back, factors, r)
        gate_back[r, :] = gate_of(first_back, third_back, gated_back, factors, r)

    by_chunk(step)
    spread(key_last, 0, key_part[...] + nt(gate_back[...], w[0, 0]) + nt(lift_back[...], w[0, 2]))
    leave(key_last, key_out.at[first])
    spread(value_last, 0, scaled(steps[0], value_part[...] + nn(hidden_back[...], w[0, 1])))
    leave(value_last, value_out.at[first])
    for copy in copies:
        copy.wait()


def local(queries, key_rows, value_rows, step_sizes, out_grads, first_saved, second_saved, third_saved):
    vectors = [a.reshape(2, TOK, DIM) for a in (queries, key_rows, value_rows)]
    matrices = [a.reshape(2, DIM, DIM) for a in (first_saved, second_saved, third_saved)]
    anywhere = pl.BlockSpec(memory_space=pl.ANY)

    def vmem(*shape, dtype=F32):
        return pltpu.VMEM(shape, dtype)

    sem = pltpu.SemaphoreType.DMA
    lines = TOK * DIM // 128
    result = pl.pallas_call(
        kernel,
        out_shape=[vmem(2 * lines, 128), vmem(lines, 128), vmem(lines, 128), *[vmem(TOK, DIM)] * 5, vmem(4, TOK, DIM),
                   vmem(2, 3, DIM, DIM, dtype=BF16)],
        in_specs=[anywhere] * 8,
        out_specs=[pl.BlockSpec(memory_space=pltpu.VMEM)] * 10,
        scratch_shapes=[
            vmem(2, TOK, DIM, dtype=BF16), vmem(2, TOK, DIM, dtype=BF16), vmem(2, TOK, DIM, dtype=BF16),
            vmem(2, 1, TOK), vmem(2, TOK, DIM, dtype=BF16),
            *[vmem(2, TOK, DIM)] * 3,
            *[vmem(2, TOK, DIM, dtype=BF16)] * 4,
            *[vmem(TOK, DIM)] * 3,
            *[vmem(TOK, DIM, dtype=BF16)] * 5,
            *[vmem(TOK, DIM, dtype=BF16)] * 3,
            vmem(3, DIM, DIM),
            vmem(2, 3, 2 * OWN, DIM), vmem(2, 3, 2 * OWN, DIM), vmem(3, 2 * OWN, DIM),
            vmem(2, 3, 2 * OWN, 128), vmem(2, 3, 2 * OWN, 128),
            vmem(4, 3, DIM, DIM, dtype=BF16),
            vmem(4, 3, 2, 2, BAND // 2, DIM, dtype=BF16),
            vmem(4, 3, 2, 2, BAND // 2, DIM, dtype=BF16),
            vmem(4, 3, 2, 2, BAND, DIM, dtype=BF16),
            vmem(4, 3, 2, BAND, DIM, dtype=BF16),
            vmem(4, 3, 2, SIDE - 1, OWN, DIM, dtype=BF16),
            vmem(3, 3, DIM, DIM, dtype=BF16),
            sem((17,)), sem((378,)), sem((378,)),
        ],
        compiler_params=pltpu.CompilerParams(
            collective_id=0, has_side_effects=True, vmem_limit_bytes=46 * 2**20
        ),
        cost_estimate=pl.CostEstimate(flops=7 * 10**9, bytes_accessed=9 * 10**6, transcendentals=10**6),
    )(*vectors, step_sizes.reshape(2, 1, TOK), out_grads.reshape(2, TOK, DIM), *matrices)
    in_vmem = pl.BlockSpec(memory_space=pltpu.VMEM)
    result = pl.pallas_call(
        last_step,
        out_shape=[jax.ShapeDtypeStruct((2 * lines, 128), F32)] * 3,
        in_specs=[in_vmem] * 11,
        out_specs=[anywhere] * 3,
        scratch_shapes=[*[vmem(TOK, DIM, dtype=BF16)] * 3, *[vmem(lines, 128)] * 2, sem((6,))],
        cost_estimate=pl.CostEstimate(flops=4 * 10**8, bytes_accessed=3 * 10**6, transcendentals=0),
        compiler_params=pltpu.CompilerParams(vmem_limit_bytes=16 * 2**20),
    )(step_sizes.reshape(2, 1, TOK), *[pltpu.with_memory_space_constraint(part, pltpu.VMEM) for part in result])
    return tuple(part.reshape(2, TOK, 1, DIM) for part in result)


def solution(mesh):
    vectors, steps, matrices = P(None, "tok", "head", None), P(None, "tok", "head"), P(None, "head", None, None)
    return jax.shard_map(
        local,
        mesh=mesh,
        in_specs=(vectors, vectors, vectors, steps, vectors, matrices, matrices, matrices),
        out_specs=(vectors, vectors, vectors),
        check_vma=False,
    )
```
